256 devices in a mesh: depth: 32 (over x_lo, z, core), tile: 8 (over x_hi, y).
Axes of the slice: x: 4 (x_hi: 2, x_lo: 2; x = x_hi * 2 + x_lo), y: 4, z: 8, core: 2. Of those that a mesh axis runs over, the one named last changes fastest.
Arguments:
- density: bfloat16 [3, 256, 16, 4096], P(None, 'depth', 'tile'), may hold values from 0 to 1
- material_weight: float32 [4, 3], replicated, may hold values from 0.3 to 3
- color_table: int32 [4, 4, 256], replicated, may hold values from 0 to 255
Outputs:
- pixels: float32 [4, 4, 16, 4096], P(None, None, 'tile', 'depth')
The draws below stay inside these ranges and needn't reach their ends.
Inputs may be any that keep to these rules, and one draw needn't show every extreme that they name: `color_table`: levels of a transfer function, 255 meaning full.
All inputs are finite; a program needn't handle non-finite values.
Results may differ from the reference program's by a relative error of at most 0.0003.
Values may be sent and summed in bfloat16 or wider, within the bound.
No kernel may reach another device: no remote copies, remote signals or barrier semaphores. Data moves between devices by JAX's collectives and lax.ppermute only.
A program may use at most 128 MiB of HBM per device.

```python
import math
import jax
import jax.numpy as jnp
from jax import lax

MATS = 3
ENERGIES = 4
BINS = 256
NX = 4096
NZ = 256
NY = 16


def touch_ends(values, rng, low, high):
    spot = [jax.random.randint(jax.random.fold_in(rng, axis), (), 0, length) for axis, length in enumerate(values.shape)]
    main_axis = values.shape.index(max(values.shape))
    next_to = spot[:main_axis] + [(spot[main_axis] + 1) % values.shape[main_axis]] + spot[main_axis + 1:]
    return values.at[tuple(spot)].set(low).at[tuple(next_to)].set(high)


def block_levels(rng, dims, pieces, smallest, high):
    level = 1.0
    for dim, shards_of in pieces:
        steps = jax.random.uniform(jax.random.fold_in(jax.random.fold_in(rng, 6), dim), (shards_of,), jnp.float32, smallest / len(pieces), high / len(pieces))
        level = level * jnp.repeat(jnp.exp(steps), dims[dim] // shards_of).reshape((-1,) + (1,) * (len(dims) - 1 - dim))
    return level


def setup_inputs(seed: int = 0) -> dict:
    arg_keys = jax.random.split(jax.random.key(seed), 4)
    return {
        "density": jnp.clip(1.0 * jax.random.uniform(arg_keys[0], (MATS, NZ, NY, NX), jnp.float32) ** block_levels(arg_keys[0], (MATS, NZ, NY, NX), ((1, 32), (2, 8)), -0.2, 0.2), 0.0, 1.0).astype(jnp.bfloat16),
        "material_weight": jnp.clip(jnp.exp(jax.random.uniform(arg_keys[1], (ENERGIES, MATS), jnp.float32, math.log(0.3), math.log(3.0))), 0.3, 3.0),
        "color_table": touch_ends(jax.random.randint(arg_keys[2], (ENERGIES, 4, BINS), 0, 256), jax.random.fold_in(arg_keys[2], 1), 0, 255).astype(jnp.int32),
    }


def shade_samples(middle, slope_z, slope_y, slope_x, material_weight, color_table, depth_total):
    highest = lax.Precision.HIGHEST
    atten = jnp.dot(material_weight, middle, precision=highest)
    grad_z = jnp.dot(material_weight, slope_z, precision=highest)
    grad_y = jnp.dot(material_weight, slope_y, precision=highest)
    grad_x = jnp.dot(material_weight, slope_x, precision=highest)
    slope_sq = grad_z * grad_z + grad_y * grad_y + grad_x * grad_x
    shading = 0.3 + 0.7 * jnp.abs(0.8 * grad_z + 0.48 * grad_y + 0.36 * grad_x) / jnp.sqrt(slope_sq + 1.0)
    gate_term = slope_sq / (1.0 + slope_sq)
    table_level = 255.0 * (1.0 - jnp.exp(-0.5 * atten))
    bin_centers = jnp.arange(color_table.shape[2], dtype=jnp.float32)[:, None]
    looked = []
    for energy in range(material_weight.shape[0]):
        hat_weights = jnp.maximum(0.0, 1.0 - jnp.abs(table_level[energy][None, :] - bin_centers)).astype(jnp.bfloat16)
        looked.append(jnp.dot(color_table[energy].astype(jnp.bfloat16), hat_weights, preferred_element_type=jnp.float32))
    colour = jnp.stack(looked) / 255.0
    opacity = colour[:, 3] * gate_term * (6.0 / depth_total)
    emission = opacity[:, None] * colour[:, :3] * shading[:, None]
    return (emission, 1.0 - opacity)

def reference(density, material_weight, color_table):
    mats, planes, height, columns = density.shape
    energies = material_weight.shape[0]
    padded = jnp.pad(density, ((0, 0), (1, 1), (1, 1), (1, 1)))

    def per_row(index):
        window = lax.dynamic_slice_in_dim(padded, index, 3, 2).astype(jnp.float32)
        middle = window[:, 1:-1, 1, 1:-1].reshape(mats, planes * columns)
        slope_z = ((window[:, 2:, 1, 1:-1] - window[:, :-2, 1, 1:-1]) * 0.5).reshape(mats, planes * columns)
        slope_y = ((window[:, 1:-1, 2, 1:-1] - window[:, 1:-1, 0, 1:-1]) * 0.5).reshape(mats, planes * columns)
        slope_x = ((window[:, 1:-1, 1, 2:] - window[:, 1:-1, 1, :-2]) * 0.5).reshape(mats, planes * columns)
        emission, transmit = shade_samples(middle, slope_z, slope_y, slope_x, material_weight, color_table, planes)
        emission = emission.reshape(energies, 3, planes, columns)
        transmit = transmit.reshape(energies, planes, columns)
        inclusive = jnp.cumprod(transmit, axis=1)
        exclusive = jnp.concatenate([jnp.ones_like(inclusive[:, :1]), inclusive[:, :-1]], axis=1)
        colour = lax.optimization_barrier(jnp.sum(exclusive[:, None] * emission, axis=2))
        return jnp.concatenate([colour, (1.0 - inclusive[:, -1])[:, None]], axis=1)
    result = lax.map(per_row, jnp.arange(height, dtype=jnp.int32))
    return result.transpose(1, 2, 0, 3)
```

```python
import functools

import jax
import jax.numpy as jnp
from jax import lax
from jax.experimental import pallas as pl
from jax.experimental.pallas import tpu as pltpu
from jax.sharding import PartitionSpec as P

LANES = 128
ROWS = 8


def shifted(axis, part, step):
    count = lax.axis_size(axis)
    pairs = [(i, i + step) for i in range(count) if 0 <= i + step < count]
    return lax.ppermute(part, axis, pairs)


def render(depth_total, weight, table, cells, above, below, front, back, out, field, slope_x):
    mats, planes, lines, blocks, _ = cells.shape
    energies = weight.shape[0]
    lane = lax.broadcasted_iota(jnp.int32, (blocks, LANES), 1)
    block = lax.broadcasted_iota(jnp.int32, (blocks, LANES), 0)
    zero = jnp.zeros((blocks, LANES), jnp.float32)

    def widen(plane, _):
        for m in range(mats):
            field[m, plane + 1, 0] = above[m, plane].astype(jnp.float32)
            field[m, plane + 1, lines + 1] = below[m, plane].astype(jnp.float32)
            for y in range(lines):
                here = cells[m, plane, y].astype(jnp.float32)
                field[m, plane + 1, y + 1] = here
                before = jnp.where(block == 0, zero, pltpu.roll(here, 1, 0))
                after = jnp.where(block == blocks - 1, zero, pltpu.roll(here, blocks - 1, 0))
                left = pltpu.roll(jnp.where(lane == LANES - 1, before, here), 1, 1)
                right = pltpu.roll(jnp.where(lane == 0, after, here), LANES - 1, 1)
                slope_x[m, plane, y] = (right - left) * 0.5
        return 0

    lax.fori_loop(0, planes, widen, 0)
    for m in range(mats):
        for y in range(lines):
            field[m, 0, y + 1] = front[m, y].astype(jnp.float32)
            field[m, planes + 1, y + 1] = back[m, y].astype(jnp.float32)

    groups = blocks // ROWS
    kinds = 4 * energies * lines

    def chunk(step, _):
        y, group = step // groups, step % groups
        rows = pl.ds(pl.multiple_of(group * ROWS, ROWS), ROWS)
        light = [[jnp.zeros((ROWS, LANES), jnp.float32) for _ in range(4)] for _ in range(energies)]
        keep = [jnp.ones((ROWS, LANES), jnp.float32) for _ in range(energies)]
        for plane in range(planes):
            middle = [field[m, plane + 1, y + 1, rows] for m in range(mats)]
            dz = [(field[m, plane + 2, y + 1, rows] - field[m, plane, y + 1, rows]) * 0.5 for m in range(mats)]
            dy = [(field[m, plane + 1, y + 2, rows] - field[m, plane + 1, y, rows]) * 0.5 for m in range(mats)]
            dx = [slope_x[m, plane, y, rows] for m in range(mats)]
            for e in range(energies):
                mix = lambda parts: sum(weight[e, m] * parts[m] for m in range(1, mats)) + weight[e, 0] * parts[0]
                grad_z, grad_y, grad_x = mix(dz), mix(dy), mix(dx)
                slope_sq = grad_z * grad_z + grad_y * grad_y + grad_x * grad_x
                root = lax.rsqrt(slope_sq + 1.0)
                shading = 0.3 + 0.7 * jnp.abs(0.8 * grad_z + 0.48 * grad_y + 0.36 * grad_x) * root
                gate = slope_sq * root * root
                level = 255.0 * (1.0 - jnp.exp(-0.5 * mix(middle)))
                bin_ = level.astype(jnp.int32)
                over = level - bin_.astype(jnp.float32)
                first = (1.0 - over).astype(jnp.bfloat16).astype(jnp.float32)
                second = over.astype(jnp.bfloat16).astype(jnp.float32)
                high = bin_ >= LANES
                spot = bin_ & (LANES - 1)

                def look(row):
                    pick = lambda r: jnp.take_along_axis(
                        jnp.broadcast_to(table[r : r + 1, :], (ROWS, LANES)), spot, axis=1, mode="promise_in_bounds"
                    )
                    return jnp.where(high, pick(row + 1), pick(row))

                here, next_ = look(4 * e), look(4 * e + 2)
                level_of = lambda word, c: (lax.shift_right_logical(word, 8 * c) & 255).astype(jnp.float32)
                hue = [first * level_of(here, c) + second * level_of(next_, c) for c in range(4)]
                opacity = hue[3] * (gate * (6.0 / (255.0 * depth_total)))
                taken = keep[e] * opacity
                keep[e] = keep[e] - taken
                lit = taken * shading
                for c in range(3):
                    light[e][c] = light[e][c] + lit * hue[c]
                light[e][3] = light[e][3] + taken
        base = group * (ROWS * kinds) + y
        for e in range(energies):
            for c in range(4):
                value = light[e][c] * (1.0 / 255.0) if c < 3 else light[e][c]
                out[pl.ds(base + (c * energies + e) * lines, ROWS, stride=kinds), :] = value
        return 0

    lax.fori_loop(0, lines * groups, chunk, 0)


def composite(parts, out):
    bricks, kinds, _ = parts.shape
    energies, channels, lines, _ = out.shape
    per = kinds // channels

    def one(brick, state):
        keep, total = state
        new = [total[c] + keep * parts[brick, c * per : (c + 1) * per, :] for c in range(channels)]
        return keep * (1.0 - parts[brick, (channels - 1) * per :, :]), tuple(new)

    zero = jnp.zeros((per, LANES), jnp.float32)
    _, total = lax.fori_loop(0, bricks, one, (zero + 1.0, (zero,) * channels))
    for c in range(channels):
        for e in range(energies):
            out[e, c] = total[c][e * lines : (e + 1) * lines, :]


def packed_table(color_table):
    energies, channels, bins = color_table.shape
    word = color_table[:, 0]
    for c in range(1, channels):
        word = word | (color_table[:, c] << (8 * c))
    after = jnp.concatenate([word[:, 1:], jnp.zeros_like(word[:, :1])], axis=1)
    return jnp.concatenate([word, after], axis=1).reshape(energies * 2 * bins // LANES, LANES)


def body(density, material_weight, color_table):
    mats, planes, lines, columns = density.shape
    energies = material_weight.shape[0]
    blocks = columns // LANES
    depth = lax.axis_size("depth")
    cells = density.reshape(mats, planes, lines, blocks, LANES)
    above = shifted("tile", cells[:, :, lines - 1], 1)
    below = shifted("tile", cells[:, :, 0], -1)
    front = shifted("depth", cells[:, planes - 1], 1)
    back = shifted("depth", cells[:, 0], -1)
    kinds = 4 * energies * lines
    vmem = pl.BlockSpec(memory_space=pltpu.VMEM)
    parts = pl.pallas_call(
        functools.partial(render, planes * depth),
        out_shape=jax.ShapeDtypeStruct((blocks * kinds, LANES), jnp.float32),
        in_specs=[pl.BlockSpec(memory_space=pltpu.SMEM)] + [vmem] * 6,
        out_specs=vmem,
        scratch_shapes=[
            pltpu.VMEM((mats, planes + 2, lines + 2, blocks, LANES), jnp.float32),
            pltpu.VMEM((mats, planes, lines, blocks, LANES), jnp.float32),
        ],
        compiler_params=pltpu.CompilerParams(vmem_limit_bytes=32 * 2**20),
        name="render",
    )(material_weight, packed_table(color_table), cells, above, below, front, back)
    parts = lax.all_to_all(parts.reshape(blocks, kinds, LANES), "depth", 0, 0, tiled=True)
    return pl.pallas_call(
        composite,
        out_shape=jax.ShapeDtypeStruct((energies, 4, lines, columns // depth), jnp.float32),
        in_specs=[vmem],
        out_specs=vmem,
        name="composite",
    )(parts)


def solution(mesh):
    return jax.shard_map(
        body,
        mesh=mesh,
        in_specs=(P(None, "depth", "tile", None), P(), P()),
        out_specs=P(None, None, "tile", "depth"),
        check_vma=False,
    )
```

```python
import functools

import jax
import jax.numpy as jnp
from jax import lax
from jax.experimental import pallas as pl
from jax.experimental.pallas import tpu as pltpu
from jax.sharding import PartitionSpec as P

LANES = 128
ROWS = 8


def facing(cells, axis, dim):
    count, last = lax.axis_size(axis), cells.shape[dim] - 1
    odd = lax.axis_index(axis) % 2
    pick = lambda at: lax.dynamic_index_in_dim(cells, at, dim, keepdims=False)
    low = [(i, i + 1) for i in range(0, count - 1, 2)]
    high = [(i, i + 1) for i in range(1, count - 1, 2)]
    both = lambda pairs: pairs + [(j, i) for i, j in pairs]
    return (
        lax.ppermute(pick(last * (1 - odd)), axis, both(low)),
        lax.ppermute(pick(last * odd), axis, both(high)),
    )


def render(depth_total, weight, table, cells, tile_a, tile_b, depth_a, depth_b, kept, sent, field, slope_x, image):
    mats, planes, lines, blocks, _ = cells.shape
    energies = weight.shape[0]
    lane = lax.broadcasted_iota(jnp.int32, (blocks, LANES), 1)
    block = lax.broadcasted_iota(jnp.int32, (blocks, LANES), 0)
    zero = jnp.zeros((blocks, LANES), jnp.float32)

    tile_odd, depth_odd = lax.axis_index("tile") % 2, lax.axis_index("depth") % 2
    beside_a = (lines + 1) * (1 - tile_odd)
    beside_b = (lines + 1) * tile_odd

    def widen(plane, _):
        for m in range(mats):
            field[m, plane + 1, beside_a] = tile_a[m, plane].astype(jnp.float32)
            field[m, plane + 1, beside_b] = tile_b[m, plane].astype(jnp.float32)
            for y in range(lines):
                here = cells[m, plane, y].astype(jnp.float32)
                field[m, plane + 1, y + 1] = here
                before = jnp.where(block == 0, zero, pltpu.roll(here, 1, 0))
                after = jnp.where(block == blocks - 1, zero, pltpu.roll(here, blocks - 1, 0))
                left = pltpu.roll(jnp.where(lane == LANES - 1, before, here), 1, 1)
                right = pltpu.roll(jnp.where(lane == 0, after, here), LANES - 1, 1)
                slope_x[m, plane, y] = (right - left) * 0.5
        return 0

    lax.fori_loop(0, planes, widen, 0)
    for m in range(mats):
        for y in range(lines):
            field[m, (planes + 1) * (1 - depth_odd), y + 1] = depth_a[m, y].astype(jnp.float32)
            field[m, (planes + 1) * depth_odd, y + 1] = depth_b[m, y].astype(jnp.float32)

    groups = blocks // ROWS
    kinds = 4 * energies * lines

    def chunk(step, _):
        y, group = step // groups, step % groups
        rows = pl.ds(pl.multiple_of(group * ROWS, ROWS), ROWS)
        light = [[jnp.zeros((ROWS, LANES), jnp.float32) for _ in range(4)] for _ in range(energies)]
        keep = [jnp.ones((ROWS, LANES), jnp.float32) for _ in range(energies)]
        for plane in range(planes):
            middle = [field[m, plane + 1, y + 1, rows] for m in range(mats)]
            dz = [(field[m, plane + 2, y + 1, rows] - field[m, plane, y + 1, rows]) * 0.5 for m in range(mats)]
            dy = [(field[m, plane + 1, y + 2, rows] - field[m, plane + 1, y, rows]) * 0.5 for m in range(mats)]
            dx = [slope_x[m, plane, y, rows] for m in range(mats)]
            for e in range(energies):
                mix = lambda parts: sum(weight[e, m] * parts[m] for m in range(1, mats)) + weight[e, 0] * parts[0]
                grad_z, grad_y, grad_x = mix(dz), mix(dy), mix(dx)
                slope_sq = grad_z * grad_z + grad_y * grad_y + grad_x * grad_x
                root = lax.rsqrt(slope_sq + 1.0)
                shading = 0.3 + 0.7 * jnp.abs(0.8 * grad_z + 0.48 * grad_y + 0.36 * grad_x) * root
                gate = slope_sq * root * root
                level = 255.0 * (1.0 - jnp.exp(-0.5 * mix(middle)))
                bin_ = level.astype(jnp.int32)
                over = level - bin_.astype(jnp.float32)
                first = (1.0 - over).astype(jnp.bfloat16).astype(jnp.float32)
                second = over.astype(jnp.bfloat16).astype(jnp.float32)
                high = bin_ >= LANES
                spot = bin_ & (LANES - 1)

                def look(row):
                    pick = lambda r: jnp.take_along_axis(
                        jnp.broadcast_to(table[r : r + 1, :], (ROWS, LANES)), spot, axis=1, mode="promise_in_bounds"
                    )
                    return jnp.where(high, pick(row + 1), pick(row))

                here, next_ = look(4 * e), look(4 * e + 2)
                level_of = lambda word, c: (lax.shift_right_logical(word, 8 * c) & 255).astype(jnp.float32)
                hue = [first * level_of(here, c) + second * level_of(next_, c) for c in range(4)]
                opacity = hue[3] * (gate * (6.0 / (255.0 * depth_total)))
                taken = keep[e] * opacity
                keep[e] = keep[e] - taken
                lit = taken * shading
                for c in range(3):
                    light[e][c] = light[e][c] + lit * hue[c]
                light[e][3] = light[e][3] + taken
        base = group * (ROWS * kinds) + y
        for e in range(energies):
            for c in range(4):
                value = light[e][c] * (1.0 / 255.0) if c < 3 else light[e][c]
                image[pl.ds(base + (c * energies + e) * lines, ROWS, stride=kinds), :] = value
        return 0

    lax.fori_loop(0, lines * groups, chunk, 0)

    def part(pair, _):
        for target, parity in ((kept, depth_odd), (sent, 1 - depth_odd)):
            start = pl.multiple_of((2 * pair + parity) * kinds, kinds)
            target[pair] = image[pl.ds(start, kinds), :]
        return 0

    lax.fori_loop(0, blocks // 2, part, 0)


def over(front, back, per):
    clear = 1.0 - front[-per:, :]
    return [front[i : i + per, :] + clear * back[i : i + per, :] for i in range(0, front.shape[0], per)]


def join(per, mine, other, out):
    odd = lax.axis_index("depth") % 2

    def one(pair, _):
        a, b = mine[pair], other[pair]
        front, back = jnp.where(odd == 0, a, b), jnp.where(odd == 0, b, a)
        for i, value in enumerate(over(front, back, per)):
            out[pair, i * per : (i + 1) * per, :] = value
        return 0

    lax.fori_loop(0, mine.shape[0], one, 0)


def composite(parts, out):
    bricks, kinds, _ = parts.shape
    energies, channels, lines, _ = out.shape
    per = kinds // channels

    keep = jnp.ones((per, LANES), jnp.float32)
    total = [jnp.zeros((per, LANES), jnp.float32) for _ in range(channels)]
    for brick in range(bricks):
        part = [parts[brick, c * per : (c + 1) * per, :] for c in range(channels)]
        total = [total[c] + keep * part[c] for c in range(channels)]
        keep = keep * (1.0 - part[channels - 1])
    for c in range(channels):
        for e in range(energies):
            out[e, c] = total[c][e * lines : (e + 1) * lines, :]


def packed_table(color_table):
    energies, channels, bins = color_table.shape
    word = color_table[:, 0]
    for c in range(1, channels):
        word = word | (color_table[:, c] << (8 * c))
    after = jnp.concatenate([word[:, 1:], jnp.zeros_like(word[:, :1])], axis=1)
    return jnp.concatenate([word, after], axis=1).reshape(energies * 2 * bins // LANES, LANES)


def body(density, material_weight, color_table):
    mats, planes, lines, columns = density.shape
    energies = material_weight.shape[0]
    blocks = columns // LANES
    depth = lax.axis_size("depth")
    cells = density.reshape(mats, planes, lines, blocks, LANES)
    tile_a, tile_b = facing(cells, "tile", 2)
    depth_a, depth_b = facing(cells, "depth", 1)
    kinds = 4 * energies * lines
    pairs = blocks // 2
    vmem = pl.BlockSpec(memory_space=pltpu.VMEM)
    half = jax.ShapeDtypeStruct((pairs, kinds, LANES), jnp.float32)
    kept, sent = pl.pallas_call(
        functools.partial(render, planes * depth),
        out_shape=(half, half),
        in_specs=[pl.BlockSpec(memory_space=pltpu.SMEM)] + [vmem] * 6,
        out_specs=(vmem, vmem),
        scratch_shapes=[
            pltpu.VMEM((mats, planes + 2, lines + 2, blocks, LANES), jnp.float32),
            pltpu.VMEM((mats, planes, lines, blocks, LANES), jnp.float32),
            pltpu.VMEM((blocks * kinds, LANES), jnp.float32),
        ],
        compiler_params=pltpu.CompilerParams(vmem_limit_bytes=32 * 2**20),
        name="render",
    )(material_weight, packed_table(color_table), cells, tile_a, tile_b, depth_a, depth_b)
    other = lax.ppermute(sent, "depth", [(i, i ^ 1) for i in range(depth)])
    joined = pl.pallas_call(
        functools.partial(join, energies * lines), out_shape=half, in_specs=[vmem, vmem], out_specs=vmem, name="join"
    )(kept, other)
    same_core = [[2 * i + c for i in range(depth // 2)] for c in range(2)]
    parts = lax.all_to_all(joined, "depth", 0, 0, axis_index_groups=same_core, tiled=True)
    return pl.pallas_call(
        composite,
        out_shape=jax.ShapeDtypeStruct((energies, 4, lines, columns // depth), jnp.float32),
        in_specs=[vmem],
        out_specs=vmem,
        name="composite",
    )(parts)


def solution(mesh):
    return jax.shard_map(
        body,
        mesh=mesh,
        in_specs=(P(None, "depth", "tile", None), P(), P()),
        out_specs=P(None, None, "tile", "depth"),
        check_vma=False,
    )
```

```python
import functools

import jax
import jax.numpy as jnp
from jax import lax
from jax.experimental import pallas as pl
from jax.experimental.pallas import tpu as pltpu
from jax.sharding import PartitionSpec as P

LANES = 128
ROWS = 8


def facing(cells, axis, dim):
    count, last = lax.axis_size(axis), cells.shape[dim] - 1
    odd = lax.axis_index(axis) % 2
    pick = lambda at: lax.dynamic_index_in_dim(cells, at, dim, keepdims=False)
    low = [(i, i + 1) for i in range(0, count - 1, 2)]
    high = [(i, i + 1) for i in range(1, count - 1, 2)]
    both = lambda pairs: pairs + [(j, i) for i, j in pairs]
    return (
        lax.ppermute(pick(last * (1 - odd)), axis, both(low)),
        lax.ppermute(pick(last * odd), axis, both(high)),
    )


def mix(weights, parts):
    total = weights[0] * parts[0]
    for weight, part in zip(weights[1:], parts[1:]):
        total = total + weight * part
    return total


def lookup(depth_total, weight, table, cells, hues, field, slope_x):
    mats, planes, lines, blocks, _ = cells.shape
    energies = weight.shape[0]
    groups = blocks // ROWS
    lane = lax.broadcasted_iota(jnp.int32, (blocks, LANES), 1)
    block = lax.broadcasted_iota(jnp.int32, (blocks, LANES), 0)
    zero = jnp.zeros((blocks, LANES), jnp.float32)

    def widen(plane, _):
        for m in range(mats):
            for y in range(lines):
                here = cells[m, plane, y].astype(jnp.float32)
                field[m, plane, y] = here
                before = jnp.where(block == 0, zero, pltpu.roll(here, 1, 0))
                after = jnp.where(block == blocks - 1, zero, pltpu.roll(here, blocks - 1, 0))
                left = pltpu.roll(jnp.where(lane == LANES - 1, before, here), 1, 1)
                right = pltpu.roll(jnp.where(lane == 0, after, here), LANES - 1, 1)
                slope_x[m, plane, y] = right - left
        return 0

    lax.fori_loop(0, planes, widen, 0)

    def chunk(step, _):
        y, group = step // groups, step % groups
        rows = pl.ds(pl.multiple_of(group * ROWS, ROWS), ROWS)
        for plane in range(planes):
            middle = [field[m, plane, y, rows] for m in range(mats)]
            for e in range(energies):
                level = 255.0 * (1.0 - jnp.exp(-0.5 * mix([weight[e, m] for m in range(mats)], middle)))
                bin_ = level.astype(jnp.int32)
                past = level - bin_.astype(jnp.float32)
                first = (1.0 - past).astype(jnp.bfloat16).astype(jnp.float32)
                second = past.astype(jnp.bfloat16).astype(jnp.float32)
                high = bin_ >= LANES
                spot = bin_ & (LANES - 1)

                def look(row):
                    pick = lambda r: jnp.take_along_axis(
                        jnp.broadcast_to(table[r : r + 1, :], (ROWS, LANES)), spot, axis=1, mode="promise_in_bounds"
                    )
                    return jnp.where(high, pick(row + 1), pick(row))

                here, next_ = look(4 * e), look(4 * e + 2)
                level_of = lambda word, c: (lax.shift_right_logical(word, 8 * c) & 255).astype(jnp.float32)
                for c in range(4):
                    hue = first * level_of(here, c) + second * level_of(next_, c)
                    hues[plane, step, 4 * e + c] = hue if c < 3 else hue * (6.0 / (255.0 * depth_total))
        return 0

    lax.fori_loop(0, lines * groups, chunk, 0)


def shade(weight, hues, field, slope_x, depth_a, depth_b, tile_a, tile_b, kept, sent, image):
    mats, planes, lines, blocks, _ = field.shape
    energies = weight.shape[0]
    groups = blocks // ROWS
    kinds = 4 * energies * lines
    tile_odd, depth_odd = lax.axis_index("tile") % 2, lax.axis_index("depth") % 2
    wide = lambda ref, *at: ref[at].astype(jnp.float32)

    def chunk(group, _):
        rows = pl.ds(pl.multiple_of(group * ROWS, ROWS), ROWS)
        for y in range(lines):
            light = [[jnp.zeros((ROWS, LANES), jnp.float32) for _ in range(4)] for _ in range(energies)]
            keep = [jnp.ones((ROWS, LANES), jnp.float32) for _ in range(energies)]
            near, far = [], []
            for m in range(mats):
                a, b = depth_a[m, y, rows], depth_b[m, y, rows]
                near.append(jnp.where(depth_odd == 1, a, b))
                far.append(jnp.where(depth_odd == 1, b, a))
            for plane in range(planes):
                dx, dy, dz = [], [], []
                for m in range(mats):
                    before = near[m] if plane == 0 else field[m, plane - 1, y, rows]
                    after = far[m] if plane == planes - 1 else field[m, plane + 1, y, rows]
                    dz.append(after - before)
                    a, b = tile_a[m, plane, rows], tile_b[m, plane, rows]
                    above = jnp.where(tile_odd == 1, a, b) if y == 0 else field[m, plane, y - 1, rows]
                    below = jnp.where(tile_odd == 1, b, a) if y == lines - 1 else field[m, plane, y + 1, rows]
                    dy.append(below - above)
                    dx.append(slope_x[m, plane, y, rows])
                for e in range(energies):
                    half = [0.5 * weight[e, m] for m in range(mats)]
                    grad_z, grad_y, grad_x = mix(half, dz), mix(half, dy), mix(half, dx)
                    slope_sq = grad_z * grad_z + grad_y * grad_y + grad_x * grad_x
                    root = lax.rsqrt(slope_sq + 1.0)
                    shading = 0.3 + jnp.abs(0.56 * grad_z + 0.336 * grad_y + 0.252 * grad_x) * root
                    hue = [hues[plane, y * groups + group, 4 * e + c] for c in range(4)]
                    taken = keep[e] * (hue[3] * (slope_sq * (root * root)))
                    keep[e] = keep[e] - taken
                    lit = taken * shading
                    for c in range(3):
                        light[e][c] = light[e][c] + lit * hue[c]
                    light[e][3] = light[e][3] + taken
            base = group * (ROWS * kinds) + y
            for e in range(energies):
                for c in range(4):
                    value = light[e][c] * (1.0 / 255.0) if c < 3 else light[e][c]
                    image[pl.ds(base + (c * energies + e) * lines, ROWS, stride=kinds), :] = value
        return 0

    lax.fori_loop(0, groups, chunk, 0)

    def part(pair, _):
        for target, parity in ((kept, depth_odd), (sent, 1 - depth_odd)):
            start = pl.multiple_of((2 * pair + parity) * kinds, kinds)
            target[pair] = image[pl.ds(start, kinds), :]
        return 0

    lax.fori_loop(0, blocks // 2, part, 0)


def join(per, mine, other, out):
    odd = lax.axis_index("depth") % 2
    for pair in range(mine.shape[0]):
        a, b = mine[pair], other[pair]
        front, back = jnp.where(odd == 0, a, b), jnp.where(odd == 0, b, a)
        clear = 1.0 - front[-per:, :]
        for i in range(0, front.shape[0], per):
            out[pair, i : i + per, :] = front[i : i + per, :] + clear * back[i : i + per, :]


def composite(parts, out):
    bricks, kinds, _ = parts.shape
    energies, channels, lines, _ = out.shape
    per = kinds // channels

    keep = jnp.ones((per, LANES), jnp.float32)
    total = [jnp.zeros((per, LANES), jnp.float32) for _ in range(channels)]
    for brick in range(bricks):
        part = [parts[brick, c * per : (c + 1) * per, :] for c in range(channels)]
        total = [total[c] + keep * part[c] for c in range(channels)]
        keep = keep * (1.0 - part[channels - 1])
    for c in range(channels):
        for e in range(energies):
            out[e, c] = total[c][e * lines : (e + 1) * lines, :]


def packed_table(color_table):
    energies, channels, bins = color_table.shape
    word = color_table[:, 0]
    for c in range(1, channels):
        word = word | (color_table[:, c] << (8 * c))
    after = jnp.concatenate([word[:, 1:], jnp.zeros_like(word[:, :1])], axis=1)
    return jnp.concatenate([word, after], axis=1).reshape(energies * 2 * bins // LANES, LANES)


def limit(mib):
    return pltpu.CompilerParams(vmem_limit_bytes=mib * 2**20)


def body(density, material_weight, color_table):
    mats, planes, lines, columns = density.shape
    energies = material_weight.shape[0]
    blocks = columns // LANES
    depth = lax.axis_size("depth")
    kinds = 4 * energies * lines
    pairs = blocks // 2
    smem, vmem = pl.BlockSpec(memory_space=pltpu.SMEM), pl.BlockSpec(memory_space=pltpu.VMEM)
    real = lambda *shape: jax.ShapeDtypeStruct(shape, jnp.float32)

    cells = density.reshape(mats, planes, lines, blocks, LANES)
    depth_a, depth_b = facing(cells, "depth", 1)
    tile_a, tile_b = facing(cells, "tile", 2)
    hues, field, slope_x = pl.pallas_call(
        functools.partial(lookup, planes * depth),
        out_shape=(
            real(planes, lines * blocks // ROWS, 4 * energies, ROWS, LANES),
            real(*cells.shape),
            real(*cells.shape),
        ),
        in_specs=[smem, vmem, vmem],
        out_specs=(vmem, vmem, vmem),
        compiler_params=limit(8),
        cost_estimate=pl.CostEstimate(flops=4_000_000_000, bytes_accessed=8_000_000, transcendentals=300_000),
        name="lookup",
    )(material_weight, packed_table(color_table), cells)
    kept, sent = pl.pallas_call(
        shade,
        out_shape=(real(pairs, kinds, LANES),) * 2,
        in_specs=[smem] + [vmem] * 7,
        out_specs=(vmem, vmem),
        scratch_shapes=[pltpu.VMEM((blocks * kinds, LANES), jnp.float32)],
        compiler_params=limit(8),
        name="shade",
    )(material_weight, hues, field, slope_x, depth_a, depth_b, tile_a, tile_b)
    other = lax.ppermute(sent, "depth", [(i, i ^ 1) for i in range(depth)])
    joined = pl.pallas_call(
        functools.partial(join, energies * lines),
        out_shape=real(pairs, kinds, LANES),
        in_specs=[vmem, vmem],
        out_specs=vmem,
        compiler_params=limit(2),
        name="join",
    )(kept, other)
    same_core = [[2 * i + c for i in range(depth // 2)] for c in range(2)]
    parts = lax.all_to_all(joined, "depth", 0, 0, axis_index_groups=same_core, tiled=True)
    return pl.pallas_call(
        composite,
        out_shape=real(energies, 4, lines, columns // depth),
        in_specs=[vmem],
        out_specs=vmem,
        compiler_params=limit(2),
        name="composite",
    )(parts)


def solution(mesh):
    return jax.shard_map(
        body,
        mesh=mesh,
        in_specs=(P(None, "depth", "tile", None), P(), P()),
        out_specs=P(None, None, "tile", "depth"),
        check_vma=False,
    )
```

```python
import functools

import jax
import jax.numpy as jnp
from jax import lax
from jax.experimental import pallas as pl
from jax.experimental.pallas import tpu as pltpu
from jax.sharding import PartitionSpec as P

LANES = 128
ROWS = 8


def partners(axis, start):
    count = lax.axis_size(axis)
    return [p for i in range(start, count - 1, 2) for p in ((i, i + 1), (i + 1, i))]


def end(axis, high, last):
    odd = lax.axis_index(axis) % 2
    return last * odd if high else last * (1 - odd)


def mix(weights, parts):
    total = weights[0] * parts[0]
    for weight, part in zip(weights[1:], parts[1:]):
        total = total + weight * part
    return total


def widen(cells, field, slope_x, low, high):
    mats, planes, lines, blocks, _ = cells.shape
    lane = lax.broadcasted_iota(jnp.int32, (blocks, LANES), 1)
    block = lax.broadcasted_iota(jnp.int32, (blocks, LANES), 0)
    zero = jnp.zeros((blocks, LANES), jnp.float32)
    for m in range(mats):
        for y in range(lines):
            low[m, y] = cells[m, end("depth", False, planes - 1), y]
            high[m, y] = cells[m, end("depth", True, planes - 1), y]

    def one(plane, _):
        for m in range(mats):
            for y in range(lines):
                here = cells[m, plane, y].astype(jnp.float32)
                field[m, plane, y] = here
                before = jnp.where(block == 0, zero, pltpu.roll(here, 1, 0))
                after = jnp.where(block == blocks - 1, zero, pltpu.roll(here, blocks - 1, 0))
                left = pltpu.roll(jnp.where(lane == LANES - 1, before, here), 1, 1)
                right = pltpu.roll(jnp.where(lane == 0, after, here), LANES - 1, 1)
                slope_x[m, plane, y] = right - left
        return 0

    lax.fori_loop(0, planes, one, 0)


def lookup(depth_total, weight, color_table, field, hues, factor, table):
    mats, planes, lines, blocks, _ = field.shape
    groups = blocks // ROWS
    energies, channels, bins = color_table.shape

    channel = lax.broadcasted_iota(jnp.int32, (channels, bins), 0)
    words = [jnp.sum(color_table[e] << (8 * channel), axis=0, keepdims=True) for e in range(energies)]
    word = jnp.concatenate(words + words[: ROWS - energies], axis=0)
    next_word = pltpu.roll(word, bins - 1, 1)
    for e in range(energies):
        for i in range(bins // LANES):
            table[4 * e + i : 4 * e + i + 1, :] = word[e : e + 1, i * LANES : (i + 1) * LANES]
            table[4 * e + 2 + i : 4 * e + 3 + i, :] = next_word[e : e + 1, i * LANES : (i + 1) * LANES]
        for m in range(mats):
            factor[mats * e + m] = jnp.broadcast_to(weight[e : e + 1, m : m + 1], (ROWS, LANES))

    def chunk(step, _):
        y, group = step // groups, step % groups
        rows = pl.ds(pl.multiple_of(group * ROWS, ROWS), ROWS)
        for plane in range(planes):
            middle = [field[m, plane, y, rows] for m in range(mats)]
            for e in range(energies):
                level = 255.0 * (1.0 - jnp.exp(-0.5 * mix([factor[mats * e + m] for m in range(mats)], middle)))
                bin_ = level.astype(jnp.int32)
                past = level - bin_.astype(jnp.float32)
                first = (1.0 - past).astype(jnp.bfloat16).astype(jnp.float32)
                second = past.astype(jnp.bfloat16).astype(jnp.float32)
                high = bin_ >= LANES
                spot = bin_ & (LANES - 1)

                def look(row):
                    pick = lambda r: jnp.take_along_axis(
                        jnp.broadcast_to(table[r : r + 1, :], (ROWS, LANES)), spot, axis=1, mode="promise_in_bounds"
                    )
                    return jnp.where(high, pick(row + 1), pick(row))

                here, next_ = look(4 * e), look(4 * e + 2)
                level_of = lambda word, c: (lax.shift_right_logical(word, 8 * c) & 255).astype(jnp.float32)
                for c in range(4):
                    hue = first * level_of(here, c) + second * level_of(next_, c)
                    hues[plane, step, 4 * e + c] = hue if c < 3 else hue * (6.0 / (255.0 * depth_total))
        return 0

    lax.fori_loop(0, lines * groups, chunk, 0)


def shade(factor, hues, field, slope_x, depth_a, depth_b, tile_a, tile_b, kept, sent, image):
    mats, planes, lines, blocks, _ = field.shape
    energies = factor.shape[0] // mats
    groups = blocks // ROWS
    kinds = 4 * energies * lines
    tile_odd, depth_odd = lax.axis_index("tile") % 2, lax.axis_index("depth") % 2

    def chunk(group, _):
        rows = pl.ds(pl.multiple_of(group * ROWS, ROWS), ROWS)
        for y in range(lines):
            light = [[jnp.zeros((ROWS, LANES), jnp.float32) for _ in range(4)] for _ in range(energies)]
            keep = [jnp.ones((ROWS, LANES), jnp.float32) for _ in range(energies)]
            near, far = [], []
            for m in range(mats):
                a, b = depth_a[m, y, rows], depth_b[m, y, rows]
                near.append(jnp.where(depth_odd == 1, a, b))
                far.append(jnp.where(depth_odd == 1, b, a))
            for plane in range(planes):
                dx, dy, dz = [], [], []
                for m in range(mats):
                    before = near[m] if plane == 0 else field[m, plane - 1, y, rows]
                    after = far[m] if plane == planes - 1 else field[m, plane + 1, y, rows]
                    dz.append(after - before)
                    a, b = tile_a[m, plane, rows], tile_b[m, plane, rows]
                    above = jnp.where(tile_odd == 1, a, b) if y == 0 else field[m, plane, y - 1, rows]
                    below = jnp.where(tile_odd == 1, b, a) if y == lines - 1 else field[m, plane, y + 1, rows]
                    dy.append(below - above)
                    dx.append(slope_x[m, plane, y, rows])
                for e in range(energies):
                    half = [0.5 * factor[mats * e + m] for m in range(mats)]
                    grad_z, grad_y, grad_x = mix(half, dz), mix(half, dy), mix(half, dx)
                    slope_sq = grad_z * grad_z + grad_y * grad_y + grad_x * grad_x
                    root = lax.rsqrt(slope_sq + 1.0)
                    shading = 0.3 + jnp.abs(0.56 * grad_z + 0.336 * grad_y + 0.252 * grad_x) * root
                    hue = [hues[plane, y * groups + group, 4 * e + c] for c in range(4)]
                    taken = keep[e] * (hue[3] * (slope_sq * (root * root)))
                    keep[e] = keep[e] - taken
                    lit = taken * shading
                    for c in range(3):
                        light[e][c] = light[e][c] + lit * hue[c]
                    light[e][3] = light[e][3] + taken
            base = group * (ROWS * kinds) + y
            for e in range(energies):
                for c in range(4):
                    value = light[e][c] * (1.0 / 255.0) if c < 3 else light[e][c]
                    image[pl.ds(base + (c * energies + e) * lines, ROWS, stride=kinds), :] = value
        return 0

    lax.fori_loop(0, groups, chunk, 0)

    def part(pair, _):
        for target, parity in ((kept, depth_odd), (sent, 1 - depth_odd)):
            start = pl.multiple_of((2 * pair + parity) * kinds, kinds)
            target[pair] = image[pl.ds(start, kinds), :]
        return 0

    lax.fori_loop(0, blocks // 2, part, 0)


def join(per, mine, other, out):
    odd = lax.axis_index("depth") % 2
    for pair in range(mine.shape[0]):
        a, b = mine[pair], other[pair]
        front, back = jnp.where(odd == 0, a, b), jnp.where(odd == 0, b, a)
        clear = 1.0 - front[-per:, :]
        for i in range(0, front.shape[0], per):
            out[pair, i : i + per, :] = front[i : i + per, :] + clear * back[i : i + per, :]


def composite(parts, out):
    bricks, kinds, _ = parts.shape
    energies, channels, lines, _ = out.shape
    per = kinds // channels

    keep = jnp.ones((per, LANES), jnp.float32)
    total = [jnp.zeros((per, LANES), jnp.float32) for _ in range(channels)]
    for brick in range(bricks):
        part = [parts[brick, c * per : (c + 1) * per, :] for c in range(channels)]
        total = [total[c] + keep * part[c] for c in range(channels)]
        keep = keep * (1.0 - part[channels - 1])
    for c in range(channels):
        for e in range(energies):
            out[e, c] = total[c][e * lines : (e + 1) * lines, :]


def limit(mib):
    return pltpu.CompilerParams(vmem_limit_bytes=mib * 2**20)


def body(density, material_weight, color_table):
    mats, planes, lines, columns = density.shape
    energies = material_weight.shape[0]
    blocks = columns // LANES
    depth = lax.axis_size("depth")
    kinds = 4 * energies * lines
    pairs = blocks // 2
    vmem = pl.BlockSpec(memory_space=pltpu.VMEM)
    real = lambda *shape: jax.ShapeDtypeStruct(shape, jnp.float32)
    short = lambda *shape: jax.ShapeDtypeStruct(shape, density.dtype)

    cells = density.reshape(mats, planes, lines, blocks, LANES)
    row = lambda high: lax.dynamic_index_in_dim(cells, end("tile", high, lines - 1), 2, keepdims=False)
    tile_a = lax.ppermute(row(False), "tile", partners("tile", 0))
    tile_b = lax.ppermute(row(True), "tile", partners("tile", 1))
    field, slope_x, low, high = pl.pallas_call(
        widen,
        out_shape=(real(*cells.shape),) * 2 + (short(mats, lines, blocks, LANES),) * 2,
        in_specs=[vmem],
        out_specs=(vmem,) * 4,
        compiler_params=limit(4),
        cost_estimate=pl.CostEstimate(flops=1_000_000_000, bytes_accessed=2_000_000, transcendentals=0),
        name="widen",
    )(cells)
    depth_a = lax.ppermute(low, "depth", partners("depth", 0))
    depth_b = lax.ppermute(high, "depth", partners("depth", 1))
    hues, factor = pl.pallas_call(
        functools.partial(lookup, planes * depth),
        out_shape=(
            real(planes, lines * blocks // ROWS, 4 * energies, ROWS, LANES),
            real(energies * mats, ROWS, LANES),
        ),
        in_specs=[vmem] * 3,
        out_specs=(vmem,) * 2,
        scratch_shapes=[pltpu.VMEM((energies * 2 * color_table.shape[2] // LANES, LANES), jnp.int32)],
        compiler_params=limit(8),
        cost_estimate=pl.CostEstimate(flops=4_000_000_000, bytes_accessed=8_000_000, transcendentals=300_000),
        name="lookup",
    )(material_weight, color_table, field)
    kept, sent = pl.pallas_call(
        shade,
        out_shape=(real(pairs, kinds, LANES),) * 2,
        in_specs=[vmem] * 8,
        out_specs=(vmem, vmem),
        scratch_shapes=[pltpu.VMEM((blocks * kinds, LANES), jnp.float32)],
        compiler_params=limit(8),
        name="shade",
    )(factor, hues, field, slope_x, depth_a, depth_b, tile_a, tile_b)
    other = lax.ppermute(sent, "depth", [(i, i ^ 1) for i in range(depth)])
    joined = pl.pallas_call(
        functools.partial(join, energies * lines),
        out_shape=real(pairs, kinds, LANES),
        in_specs=[vmem, vmem],
        out_specs=vmem,
        compiler_params=limit(2),
        name="join",
    )(kept, other)
    same_core = [[2 * i + c for i in range(depth // 2)] for c in range(2)]
    parts = lax.all_to_all(joined, "depth", 0, 0, axis_index_groups=same_core, tiled=True)
    return pl.pallas_call(
        composite,
        out_shape=real(energies, 4, lines, columns // depth),
        in_specs=[vmem],
        out_specs=vmem,
        compiler_params=limit(2),
        name="composite",
    )(parts)


def solution(mesh):
    return jax.shard_map(
        body,
        mesh=mesh,
        in_specs=(P(None, "depth", "tile", None), P(), P()),
        out_specs=P(None, None, "tile", "depth"),
        check_vma=False,
    )
```

```python
import functools

import jax
import jax.numpy as jnp
from jax import lax
from jax.experimental import pallas as pl
from jax.experimental.pallas import tpu as pltpu
from jax.sharding import PartitionSpec as P

LANES = 128
ROWS = 8


def partners(axis, start):
    count = lax.axis_size(axis)
    return [p for i in range(start, count - 1, 2) for p in ((i, i + 1), (i + 1, i))]


def end(axis, high, last):
    odd = lax.axis_index(axis) % 2
    return last * odd if high else last * (1 - odd)


def mix(weights, parts):
    total = weights[0] * parts[0]
    for weight, part in zip(weights[1:], parts[1:]):
        total = total + weight * part
    return total


def widen(cells, field, slope_x, low, high):
    mats, planes, lines, blocks, _ = cells.shape
    lane = lax.broadcasted_iota(jnp.int32, (blocks, LANES), 1)
    block = lax.broadcasted_iota(jnp.int32, (blocks, LANES), 0)
    zero = jnp.zeros((blocks, LANES), jnp.float32)
    for m in range(mats):
        for y in range(lines):
            low[m, y] = cells[m, end("depth", False, planes - 1), y]
            high[m, y] = cells[m, end("depth", True, planes - 1), y]

    def one(plane, _):
        for m in range(mats):
            for y in range(lines):
                here = cells[m, plane, y].astype(jnp.float32)
                field[m, plane, y] = here
                before = jnp.where(block == 0, zero, pltpu.roll(here, 1, 0))
                after = jnp.where(block == blocks - 1, zero, pltpu.roll(here, blocks - 1, 0))
                left = pltpu.roll(jnp.where(lane == LANES - 1, before, here), 1, 1)
                right = pltpu.roll(jnp.where(lane == 0, after, here), LANES - 1, 1)
                slope_x[m, plane, y] = right - left
        return 0

    lax.fori_loop(0, planes, one, 0)


def lookup(depth_total, weight, color_table, field, hues, factor, table):
    mats, planes, lines, blocks, _ = field.shape
    groups = blocks // ROWS
    energies, channels, bins = color_table.shape

    channel = lax.broadcasted_iota(jnp.int32, (channels, bins), 0)
    words = [jnp.sum(color_table[e] << (8 * channel), axis=0, keepdims=True) for e in range(energies)]
    word = jnp.concatenate(words + words[: ROWS - energies], axis=0)
    next_word = pltpu.roll(word, bins - 1, 1)
    for e in range(energies):
        for i in range(bins // LANES):
            table[4 * e + i : 4 * e + i + 1, :] = word[e : e + 1, i * LANES : (i + 1) * LANES]
            table[4 * e + 2 + i : 4 * e + 3 + i, :] = next_word[e : e + 1, i * LANES : (i + 1) * LANES]
        for m in range(mats):
            factor[mats * e + m] = jnp.broadcast_to(weight[e : e + 1, m : m + 1], (ROWS, LANES))

    def chunk(step, _):
        y, group = step // groups, step % groups
        rows = pl.ds(pl.multiple_of(group * ROWS, ROWS), ROWS)
        for plane in range(planes):
            middle = [field[m, plane, y, rows] for m in range(mats)]
            for e in range(energies):
                level = 255.0 * (1.0 - jnp.exp(-0.5 * mix([factor[mats * e + m] for m in range(mats)], middle)))
                bin_ = level.astype(jnp.int32)
                past = level - bin_.astype(jnp.float32)
                first = (1.0 - past).astype(jnp.bfloat16).astype(jnp.float32)
                second = past.astype(jnp.bfloat16).astype(jnp.float32)
                high = bin_ >= LANES
                spot = bin_ & (LANES - 1)

                def look(row):
                    pick = lambda r: jnp.take_along_axis(
                        jnp.broadcast_to(table[r : r + 1, :], (ROWS, LANES)), spot, axis=1, mode="promise_in_bounds"
                    )
                    return jnp.where(high, pick(row + 1), pick(row))

                here, next_ = look(4 * e), look(4 * e + 2)
                level_of = lambda word, c: (lax.shift_right_logical(word, 8 * c) & 255).astype(jnp.float32)
                for c in range(4):
                    hue = first * level_of(here, c) + second * level_of(next_, c)
                    hues[plane, step, 4 * e + c] = hue if c < 3 else hue * (6.0 / (255.0 * depth_total))
        return 0

    lax.fori_loop(0, lines * groups, chunk, 0)


def shade(factor, hues, field, slope_x, depth_a, depth_b, tile_a, tile_b, kept, sent, image):
    mats, planes, lines, blocks, _ = field.shape
    energies = factor.shape[0] // mats
    groups = blocks // ROWS
    kinds = 4 * energies * lines
    tile_odd, depth_odd = lax.axis_index("tile") % 2, lax.axis_index("depth") % 2

    def chunk(group, _):
        rows = pl.ds(pl.multiple_of(group * ROWS, ROWS), ROWS)
        for y in range(lines):
            light = [[jnp.zeros((ROWS, LANES), jnp.float32) for _ in range(4)] for _ in range(energies)]
            keep = [jnp.ones((ROWS, LANES), jnp.float32) for _ in range(energies)]
            near, far = [], []
            for m in range(mats):
                a, b = depth_a[m, y, rows], depth_b[m, y, rows]
                near.append(jnp.where(depth_odd == 1, a, b))
                far.append(jnp.where(depth_odd == 1, b, a))
            for plane in range(planes):
                dx, dy, dz = [], [], []
                for m in range(mats):
                    before = near[m] if plane == 0 else field[m, plane - 1, y, rows]
                    after = far[m] if plane == planes - 1 else field[m, plane + 1, y, rows]
                    dz.append(after - before)
                    a, b = tile_a[m, plane, rows], tile_b[m, plane, rows]
                    above = jnp.where(tile_odd == 1, a, b) if y == 0 else field[m, plane, y - 1, rows]
                    below = jnp.where(tile_odd == 1, b, a) if y == lines - 1 else field[m, plane, y + 1, rows]
                    dy.append(below - above)
                    dx.append(slope_x[m, plane, y, rows])
                for e in range(energies):
                    half = [0.5 * factor[mats * e + m] for m in range(mats)]
                    grad_z, grad_y, grad_x = mix(half, dz), mix(half, dy), mix(half, dx)
                    slope_sq = grad_z * grad_z + grad_y * grad_y + grad_x * grad_x
                    root = lax.rsqrt(slope_sq + 1.0)
                    shading = 0.3 + jnp.abs(0.56 * grad_z + 0.336 * grad_y + 0.252 * grad_x) * root
                    hue = [hues[plane, y * groups + group, 4 * e + c] for c in range(4)]
                    taken = keep[e] * (hue[3] * (slope_sq * (root * root)))
                    keep[e] = keep[e] - taken
                    lit = taken * shading
                    for c in range(3):
                        light[e][c] = light[e][c] + lit * hue[c]
                    light[e][3] = light[e][3] + taken
            base = group * (ROWS * kinds) + y
            for e in range(energies):
                for c in range(4):
                    value = light[e][c] * (1.0 / 255.0) if c < 3 else light[e][c]
                    image[pl.ds(base + (c * energies + e) * lines, ROWS, stride=kinds), :] = value
        return 0

    lax.fori_loop(0, groups, chunk, 0)

    def part(pair, _):
        for target, parity in ((kept, depth_odd), (sent, 1 - depth_odd)):
            start = pl.multiple_of((2 * pair + parity) * kinds, kinds)
            target[pair] = image[pl.ds(start, kinds), :]
        return 0

    lax.fori_loop(0, blocks // 2, part, 0)


FINE, COARSE, TOP, KNEE = 1500.0, 64.0, 32767.0, 40.0
BEND = TOP - FINE * (KNEE - 1.0)
NOTHING = -32768


def encode(value):
    octave = jnp.log2(jnp.maximum(value, 1e-37))
    code = jnp.maximum(TOP + FINE * (octave + 1.0), BEND + COARSE * (octave + KNEE))
    code = jnp.round(jnp.minimum(code, TOP)).astype(jnp.int32)
    return jnp.where(value > 1e-37, code, NOTHING).astype(jnp.int16)


def decode(code):
    code = code.astype(jnp.int32)
    wide = code.astype(jnp.float32)
    octave = jnp.minimum((wide - TOP) * (1.0 / FINE) - 1.0, (wide - BEND) * (1.0 / COARSE) - KNEE)
    return jnp.where(code > NOTHING, jnp.exp2(octave), 0.0)


def join(per, mine, other, out):
    odd = lax.axis_index("depth") % 2
    for pair in range(mine.shape[0]):
        a, b = mine[pair], other[pair]
        front, back = jnp.where(odd == 0, a, b), jnp.where(odd == 0, b, a)
        clear = 1.0 - front[-per:, :]
        both = [front[i : i + per, :] + clear * back[i : i + per, :] for i in range(0, front.shape[0], per)]
        out[pair] = encode(jnp.concatenate(both, axis=0))


def composite(parts, out):
    bricks, kinds, _ = parts.shape
    energies, channels, lines, _ = out.shape
    per = kinds // channels

    keep = jnp.ones((per, LANES), jnp.float32)
    total = [jnp.zeros((per, LANES), jnp.float32) for _ in range(channels)]
    for brick in range(bricks):
        part = decode(parts[brick])
        for c in range(channels):
            total[c] = total[c] + keep * part[c * per : (c + 1) * per, :]
        keep = keep * (1.0 - part[(channels - 1) * per :, :])
    for c in range(channels):
        for e in range(energies):
            out[e, c] = total[c][e * lines : (e + 1) * lines, :]


def limit(mib):
    return pltpu.CompilerParams(vmem_limit_bytes=mib * 2**20)


def body(density, material_weight, color_table):
    mats, planes, lines, columns = density.shape
    energies = material_weight.shape[0]
    blocks = columns // LANES
    depth = lax.axis_size("depth")
    kinds = 4 * energies * lines
    pairs = blocks // 2
    vmem = pl.BlockSpec(memory_space=pltpu.VMEM)
    real = lambda *shape: jax.ShapeDtypeStruct(shape, jnp.float32)
    short = lambda *shape: jax.ShapeDtypeStruct(shape, density.dtype)

    cells = density.reshape(mats, planes, lines, blocks, LANES)
    row = lambda high: lax.dynamic_index_in_dim(cells, end("tile", high, lines - 1), 2, keepdims=False)
    tile_a = lax.ppermute(row(False), "tile", partners("tile", 0))
    tile_b = lax.ppermute(row(True), "tile", partners("tile", 1))
    field, slope_x, low, high = pl.pallas_call(
        widen,
        out_shape=(real(*cells.shape),) * 2 + (short(mats, lines, blocks, LANES),) * 2,
        in_specs=[vmem],
        out_specs=(vmem,) * 4,
        compiler_params=limit(4),
        cost_estimate=pl.CostEstimate(flops=1_000_000_000, bytes_accessed=2_000_000, transcendentals=0),
        name="widen",
    )(cells)
    depth_a = lax.ppermute(low, "depth", partners("depth", 0))
    depth_b = lax.ppermute(high, "depth", partners("depth", 1))
    hues, factor = pl.pallas_call(
        functools.partial(lookup, planes * depth),
        out_shape=(
            real(planes, lines * blocks // ROWS, 4 * energies, ROWS, LANES),
            real(energies * mats, ROWS, LANES),
        ),
        in_specs=[vmem] * 3,
        out_specs=(vmem,) * 2,
        scratch_shapes=[pltpu.VMEM((energies * 2 * color_table.shape[2] // LANES, LANES), jnp.int32)],
        compiler_params=limit(8),
        cost_estimate=pl.CostEstimate(flops=4_000_000_000, bytes_accessed=8_000_000, transcendentals=300_000),
        name="lookup",
    )(material_weight, color_table, field)
    kept, sent = pl.pallas_call(
        shade,
        out_shape=(real(pairs, kinds, LANES),) * 2,
        in_specs=[vmem] * 8,
        out_specs=(vmem, vmem),
        scratch_shapes=[pltpu.VMEM((blocks * kinds, LANES), jnp.float32)],
        compiler_params=limit(8),
        name="shade",
    )(factor, hues, field, slope_x, depth_a, depth_b, tile_a, tile_b)
    other = lax.ppermute(sent, "depth", [(i, i ^ 1) for i in range(depth)])
    joined = pl.pallas_call(
        functools.partial(join, energies * lines),
        out_shape=jax.ShapeDtypeStruct((pairs, kinds, LANES), jnp.int16),
        in_specs=[vmem, vmem],
        out_specs=vmem,
        compiler_params=limit(2),
        name="join",
    )(kept, other)
    same_core = [[2 * i + c for i in range(depth // 2)] for c in range(2)]
    parts = lax.all_to_all(joined, "depth", 0, 0, axis_index_groups=same_core, tiled=True)
    return pl.pallas_call(
        composite,
        out_shape=real(energies, 4, lines, columns // depth),
        in_specs=[vmem],
        out_specs=vmem,
        compiler_params=limit(2),
        name="composite",
    )(parts)


def solution(mesh):
    return jax.shard_map(
        body,
        mesh=mesh,
        in_specs=(P(None, "depth", "tile", None), P(), P()),
        out_specs=P(None, None, "tile", "depth"),
        check_vma=False,
    )
```

```python
import functools
import math

import jax
import jax.numpy as jnp
from jax import lax
from jax.experimental import pallas as pl
from jax.experimental.pallas import tpu as pltpu
from jax.sharding import PartitionSpec as P

LANES = 128
ROWS = 8


def partners(axis, start):
    count = lax.axis_size(axis)
    return [p for i in range(start, count - 1, 2) for p in ((i, i + 1), (i + 1, i))]


def end(axis, high, last):
    odd = lax.axis_index(axis) % 2
    return last * odd if high else last * (1 - odd)


def mix(weights, parts):
    total = weights[0] * parts[0]
    for weight, part in zip(weights[1:], parts[1:]):
        total = total + weight * part
    return total


def plane_to_send(high, cells, *refs):
    mats, planes, lines, _, _ = cells.shape
    for m in range(mats):
        for y in range(lines):
            refs[-1][m, y] = cells[m, end("depth", high, planes - 1), y]


def rounded(x):
    big = x * 65537.0
    return big - (big - x)


def lookup(depth_total, weight, color_table, cells, hues, field, slope_x, half, power, even, odd):
    mats, planes, lines, blocks, _ = cells.shape
    groups = blocks // ROWS
    energies, channels, bins = color_table.shape

    channel = lax.broadcasted_iota(jnp.int32, (channels, bins), 0)
    words = [jnp.sum(color_table[e] << (8 * channel), axis=0, keepdims=True) for e in range(energies)]
    word = jnp.concatenate(words + words[: ROWS - energies], axis=0)
    place = lax.broadcasted_iota(jnp.int32, (ROWS, LANES), 1)
    twice = (2 * place) & (LANES - 1)
    pick = lambda row, spot: jnp.take_along_axis(row, spot, axis=1, mode="promise_in_bounds")
    for table, spot in ((even, twice), (odd, twice + 1)):
        table[...] = jnp.where(place < LANES // 2, pick(word[:, :LANES], spot), pick(word[:, LANES:], spot))
    for e in range(energies):
        for m in range(mats):
            value = 0.5 * jnp.broadcast_to(weight[e : e + 1, m : m + 1], (ROWS, LANES))
            half[mats * e + m] = value
            power[mats * e + m] = value * (-math.log2(math.e))

    lane = lax.broadcasted_iota(jnp.int32, (blocks, LANES), 1)
    block = lax.broadcasted_iota(jnp.int32, (blocks, LANES), 0)
    zero = jnp.zeros((blocks, LANES), jnp.float32)

    def line(step, _):
        plane, y = step // lines, step % lines
        here = [cells[m, plane, y].astype(jnp.float32) for m in range(mats)]
        for m in range(mats):
            field[m, plane, y] = here[m]
            before = jnp.where(block == 0, zero, pltpu.roll(here[m], 1, 0))
            after = jnp.where(block == blocks - 1, zero, pltpu.roll(here[m], blocks - 1, 0))
            left = pltpu.roll(jnp.where(lane == LANES - 1, before, here[m]), 1, 1)
            right = pltpu.roll(jnp.where(lane == 0, after, here[m]), LANES - 1, 1)
            slope_x[m, plane, y] = right - left
        for group in range(groups):
            middle = [here[m][group * ROWS : (group + 1) * ROWS] for m in range(mats)]
            for e in range(energies):
                fall = jnp.exp2(mix([power[mats * e + m] for m in range(mats)], middle))
                level = 127.5 - 127.5 * fall
                next_even = (level + 0.5).astype(jnp.int32)
                away = jnp.abs(level - next_even.astype(jnp.float32))
                away = away + away
                at_odd, at_even = rounded(away), rounded(1.0 - away)
                word_odd = pick(jnp.broadcast_to(odd[e : e + 1, :], (ROWS, LANES)), level.astype(jnp.int32))
                word_even = pick(jnp.broadcast_to(even[e : e + 1, :], (ROWS, LANES)), next_even)
                level_of = lambda word, c: (lax.shift_right_logical(word, 8 * c) & 255).astype(jnp.float32)
                for c in range(4):
                    hue = at_even * level_of(word_even, c) + at_odd * level_of(word_odd, c)
                    hues[plane, y * groups + group, 4 * e + c] = hue if c < 3 else hue * (6.0 / (255.0 * depth_total))
        return 0

    lax.fori_loop(0, planes * lines, line, 0)


def shade(half, hues, field, slope_x, depth_a, depth_b, tile_a, tile_b, kept, sent, image):
    mats, planes, lines, blocks, _ = field.shape
    energies = half.shape[0] // mats
    groups = blocks // ROWS
    kinds = 4 * energies * lines
    tile_odd, depth_odd = lax.axis_index("tile") % 2, lax.axis_index("depth") % 2

    def chunk(group, _):
        rows = pl.ds(pl.multiple_of(group * ROWS, ROWS), ROWS)
        for y in range(lines):
            light = [[jnp.zeros((ROWS, LANES), jnp.float32) for _ in range(4)] for _ in range(energies)]
            keep = [jnp.ones((ROWS, LANES), jnp.float32) for _ in range(energies)]
            near, far = [], []
            for m in range(mats):
                a, b = depth_a[m, y, rows], depth_b[m, y, rows]
                near.append(jnp.where(depth_odd == 1, a, b))
                far.append(jnp.where(depth_odd == 1, b, a))
            for plane in range(planes):
                dx, dy, dz = [], [], []
                for m in range(mats):
                    before = near[m] if plane == 0 else field[m, plane - 1, y, rows]
                    after = far[m] if plane == planes - 1 else field[m, plane + 1, y, rows]
                    dz.append(after - before)
                    a, b = tile_a[m, plane, rows], tile_b[m, plane, rows]
                    above = jnp.where(tile_odd == 1, a, b) if y == 0 else field[m, plane, y - 1, rows]
                    below = jnp.where(tile_odd == 1, b, a) if y == lines - 1 else field[m, plane, y + 1, rows]
                    dy.append(below - above)
                    dx.append(slope_x[m, plane, y, rows])
                for e in range(energies):
                    share = [half[mats * e + m] for m in range(mats)]
                    grad_z, grad_y, grad_x = mix(share, dz), mix(share, dy), mix(share, dx)
                    slope_sq = grad_z * grad_z + grad_y * grad_y + grad_x * grad_x
                    root = lax.rsqrt(slope_sq + 1.0)
                    shading = 0.3 + jnp.abs(0.56 * grad_z + 0.336 * grad_y + 0.252 * grad_x) * root
                    hue = [hues[plane, y * groups + group, 4 * e + c] for c in range(4)]
                    taken = keep[e] * (hue[3] * (slope_sq * (root * root)))
                    keep[e] = keep[e] - taken
                    lit = taken * shading
                    for c in range(3):
                        light[e][c] = light[e][c] + lit * hue[c]
                    light[e][3] = light[e][3] + taken
            base = group * (ROWS * kinds) + y
            for e in range(energies):
                for c in range(4):
                    value = light[e][c] * (1.0 / 255.0) if c < 3 else light[e][c]
                    image[pl.ds(base + (c * energies + e) * lines, ROWS, stride=kinds), :] = value
        return 0

    lax.fori_loop(0, groups, chunk, 0)

    def part(pair, _):
        for target, parity in ((kept, depth_odd), (sent, 1 - depth_odd)):
            start = pl.multiple_of((2 * pair + parity) * kinds, kinds)
            target[pair] = image[pl.ds(start, kinds), :]
        return 0

    lax.fori_loop(0, blocks // 2, part, 0)


FINE, COARSE, TOP, KNEE = 1500.0, 64.0, 32767.0, 40.0
BEND = TOP - FINE * (KNEE - 1.0)
NOTHING = -32768


def encode(value):
    octave = jnp.log2(jnp.maximum(value, 1e-37))
    code = jnp.maximum(TOP + FINE * (octave + 1.0), BEND + COARSE * (octave + KNEE))
    code = jnp.round(jnp.minimum(code, TOP)).astype(jnp.int32)
    return jnp.where(value > 1e-37, code, NOTHING).astype(jnp.int16)


def decode(code):
    code = code.astype(jnp.int32)
    wide = code.astype(jnp.float32)
    octave = jnp.minimum((wide - TOP) * (1.0 / FINE) - 1.0, (wide - BEND) * (1.0 / COARSE) - KNEE)
    return jnp.where(code > NOTHING, jnp.exp2(octave), 0.0)


def join(per, mine, other, out):
    odd = lax.axis_index("depth") % 2
    for pair in range(mine.shape[0]):
        a, b = mine[pair], other[pair]
        front, back = jnp.where(odd == 0, a, b), jnp.where(odd == 0, b, a)
        clear = 1.0 - front[-per:, :]
        both = [front[i : i + per, :] + clear * back[i : i + per, :] for i in range(0, front.shape[0], per)]
        out[pair] = encode(jnp.concatenate(both, axis=0))


def composite(parts, out):
    bricks, kinds, _ = parts.shape
    energies, channels, lines, _ = out.shape
    per = kinds // channels

    keep = jnp.ones((per, LANES), jnp.float32)
    total = [jnp.zeros((per, LANES), jnp.float32) for _ in range(channels)]
    for brick in range(bricks):
        part = decode(parts[brick])
        for c in range(channels):
            total[c] = total[c] + keep * part[c * per : (c + 1) * per, :]
        keep = keep * (1.0 - part[(channels - 1) * per :, :])
    for c in range(channels):
        for e in range(energies):
            out[e, c] = total[c][e * lines : (e + 1) * lines, :]


def limit(mib):
    return pltpu.CompilerParams(vmem_limit_bytes=mib * 2**20)


def body(density, material_weight, color_table):
    mats, planes, lines, columns = density.shape
    energies = material_weight.shape[0]
    blocks = columns // LANES
    depth = lax.axis_size("depth")
    kinds = 4 * energies * lines
    pairs = blocks // 2
    vmem = pl.BlockSpec(memory_space=pltpu.VMEM)
    real = lambda *shape: jax.ShapeDtypeStruct(shape, jnp.float32)
    short = lambda *shape: jax.ShapeDtypeStruct(shape, density.dtype)

    cells = density.reshape(mats, planes, lines, blocks, LANES)
    rows = [lax.dynamic_index_in_dim(cells, end("tile", high, lines - 1), 2, keepdims=False) for high in (False, True)]
    tile_a = lax.ppermute(rows[0], "tile", partners("tile", 0))
    tile_b = lax.ppermute(rows[1], "tile", partners("tile", 1))

    def send(high, *before):
        return pl.pallas_call(
            functools.partial(plane_to_send, high),
            out_shape=short(mats, lines, blocks, LANES),
            in_specs=[vmem] + [pl.BlockSpec(memory_space=pl.ANY)] * len(before),
            out_specs=vmem,
            compiler_params=limit(2),
            cost_estimate=pl.CostEstimate(flops=1_000_000_000, bytes_accessed=2_000_000, transcendentals=0),
            name="plane_to_send",
        )(cells, *before)

    plane_b = send(True, *rows)
    depth_b = lax.ppermute(plane_b, "depth", partners("depth", 1))
    depth_a = lax.ppermute(send(False, plane_b), "depth", partners("depth", 0))
    hues, field, slope_x, half = pl.pallas_call(
        functools.partial(lookup, planes * depth),
        out_shape=(
            real(planes, lines * blocks // ROWS, 4 * energies, ROWS, LANES),
            real(*cells.shape),
            real(*cells.shape),
            real(energies * mats, ROWS, LANES),
        ),
        in_specs=[vmem] * 3,
        out_specs=(vmem,) * 4,
        scratch_shapes=[
            pltpu.VMEM((energies * mats, ROWS, LANES), jnp.float32),
            pltpu.VMEM((ROWS, LANES), jnp.int32),
            pltpu.VMEM((ROWS, LANES), jnp.int32),
        ],
        compiler_params=limit(8),
        cost_estimate=pl.CostEstimate(flops=4_000_000_000, bytes_accessed=8_000_000, transcendentals=300_000),
        name="lookup",
    )(material_weight, color_table, cells)
    kept, sent = pl.pallas_call(
        shade,
        out_shape=(real(pairs, kinds, LANES),) * 2,
        in_specs=[vmem] * 8,
        out_specs=(vmem, vmem),
        scratch_shapes=[pltpu.VMEM((blocks * kinds, LANES), jnp.float32)],
        compiler_params=limit(8),
        name="shade",
    )(half, hues, field, slope_x, depth_a, depth_b, tile_a, tile_b)
    other = lax.ppermute(sent, "depth", [(i, i ^ 1) for i in range(depth)])
    joined = pl.pallas_call(
        functools.partial(join, energies * lines),
        out_shape=jax.ShapeDtypeStruct((pairs, kinds, LANES), jnp.int16),
        in_specs=[vmem, vmem],
        out_specs=vmem,
        compiler_params=limit(2),
        name="join",
    )(kept, other)
    same_core = [[2 * i + c for i in range(depth // 2)] for c in range(2)]
    parts = lax.all_to_all(joined, "depth", 0, 0, axis_index_groups=same_core, tiled=True)
    return pl.pallas_call(
        composite,
        out_shape=real(energies, 4, lines, columns // depth),
        in_specs=[vmem],
        out_specs=vmem,
        compiler_params=limit(2),
        name="composite",
    )(parts)


def solution(mesh):
    return jax.shard_map(
        body,
        mesh=mesh,
        in_specs=(P(None, "depth", "tile", None), P(), P()),
        out_specs=P(None, None, "tile", "depth"),
        check_vma=False,
    )
```

```python
import functools
import math

import jax
import jax.numpy as jnp
from jax import lax
from jax.experimental import pallas as pl
from jax.experimental.pallas import tpu as pltpu
from jax.sharding import PartitionSpec as P

LANES = 128
ROWS = 8


def partners(axis, start):
    count = lax.axis_size(axis)
    ends = [(0, count - 1), (count - 1, 0)] if start else []
    return ends + [p for i in range(start, count - 1, 2) for p in ((i, i + 1), (i + 1, i))]


def inside(axis):
    place = lax.axis_index(axis)
    return (place > 0) & (place < lax.axis_size(axis) - 1)


def end(axis, high, last):
    odd = lax.axis_index(axis) % 2
    return last * odd if high else last * (1 - odd)


def mix(weights, parts):
    total = weights[0] * parts[0]
    for weight, part in zip(weights[1:], parts[1:]):
        total = total + weight * part
    return total


def plane_to_send(high, cells, *refs):
    mats, planes, lines, _, _ = cells.shape
    for m in range(mats):
        for y in range(lines):
            refs[-1][m, y] = cells[m, end("depth", high, planes - 1), y]


def rounded(x):
    big = x * 65537.0
    return big - (big - x)


def lookup(depth_total, weight, color_table, cells, hues, field, slope_x, half, power, even, odd):
    mats, planes, lines, blocks, _ = cells.shape
    groups = blocks // ROWS
    energies, channels, bins = color_table.shape

    channel = lax.broadcasted_iota(jnp.int32, (channels, bins), 0)
    words = [jnp.sum(color_table[e] << (8 * channel), axis=0, keepdims=True) for e in range(energies)]
    word = jnp.concatenate(words + words[: ROWS - energies], axis=0)
    place = lax.broadcasted_iota(jnp.int32, (ROWS, LANES), 1)
    twice = (2 * place) & (LANES - 1)
    pick = lambda row, spot: jnp.take_along_axis(row, spot, axis=1, mode="promise_in_bounds")
    for table, spot in ((even, twice), (odd, twice + 1)):
        table[...] = jnp.where(place < LANES // 2, pick(word[:, :LANES], spot), pick(word[:, LANES:], spot))
    for e in range(energies):
        for m in range(mats):
            value = 0.5 * jnp.broadcast_to(weight[e : e + 1, m : m + 1], (ROWS, LANES))
            half[mats * e + m] = value
            power[mats * e + m] = value * (-math.log2(math.e))

    lane = lax.broadcasted_iota(jnp.int32, (blocks, LANES), 1)
    block = lax.broadcasted_iota(jnp.int32, (blocks, LANES), 0)
    zero = jnp.zeros((blocks, LANES), jnp.float32)

    def line(step, _):
        plane, y = step // lines, step % lines
        here = [cells[m, plane, y].astype(jnp.float32) for m in range(mats)]
        for m in range(mats):
            field[m, plane, y] = here[m]
            before = jnp.where(block == 0, zero, pltpu.roll(here[m], 1, 0))
            after = jnp.where(block == blocks - 1, zero, pltpu.roll(here[m], blocks - 1, 0))
            left = pltpu.roll(jnp.where(lane == LANES - 1, before, here[m]), 1, 1)
            right = pltpu.roll(jnp.where(lane == 0, after, here[m]), LANES - 1, 1)
            slope_x[m, plane, y] = right - left
        for group in range(groups):
            middle = [here[m][group * ROWS : (group + 1) * ROWS] for m in range(mats)]
            for e in range(energies):
                fall = jnp.exp2(mix([power[mats * e + m] for m in range(mats)], middle))
                level = 127.5 - 127.5 * fall
                next_even = (level + 0.5).astype(jnp.int32)
                away = jnp.abs(level - next_even.astype(jnp.float32))
                away = away + away
                at_odd, at_even = rounded(away), rounded(1.0 - away)
                word_odd = pick(jnp.broadcast_to(odd[e : e + 1, :], (ROWS, LANES)), level.astype(jnp.int32))
                word_even = pick(jnp.broadcast_to(even[e : e + 1, :], (ROWS, LANES)), next_even)
                level_of = lambda word, c: (lax.shift_right_logical(word, 8 * c) & 255).astype(jnp.float32)
                for c in range(4):
                    hue = at_even * level_of(word_even, c) + at_odd * level_of(word_odd, c)
                    hues[plane, y * groups + group, 4 * e + c] = hue if c < 3 else hue * (6.0 / (255.0 * depth_total))
        return 0

    lax.fori_loop(0, planes * lines, line, 0, unroll=4)


def shade(half, hues, field, slope_x, depth_a, depth_b, tile_a, tile_b, kept, sent, image):
    mats, planes, lines, blocks, _ = field.shape
    energies = half.shape[0] // mats
    groups = blocks // ROWS
    kinds = 4 * energies * lines
    pitch = image.shape[0] // blocks
    tile_odd, depth_odd = lax.axis_index("tile") % 2, lax.axis_index("depth") % 2
    tile_inside, depth_inside = inside("tile"), inside("depth")

    def chunk(group, _):
        rows = pl.ds(pl.multiple_of(group * ROWS, ROWS), ROWS)
        for y in range(lines):
            light = [[jnp.zeros((ROWS, LANES), jnp.float32) for _ in range(4)] for _ in range(energies)]
            keep = [jnp.ones((ROWS, LANES), jnp.float32) for _ in range(energies)]
            near, far = [], []
            for m in range(mats):
                a, b = depth_a[m, y, rows], depth_b[m, y, rows]
                b = jnp.where(depth_inside, b, jnp.zeros_like(b))
                near.append(jnp.where(depth_odd == 1, a, b))
                far.append(jnp.where(depth_odd == 1, b, a))
            for plane in range(planes):
                dx, dy, dz = [], [], []
                for m in range(mats):
                    before = near[m] if plane == 0 else field[m, plane - 1, y, rows]
                    after = far[m] if plane == planes - 1 else field[m, plane + 1, y, rows]
                    dz.append(after - before)
                    a, b = tile_a[m, plane, rows], tile_b[m, plane, rows]
                    b = jnp.where(tile_inside, b, jnp.zeros_like(b))
                    above = jnp.where(tile_odd == 1, a, b) if y == 0 else field[m, plane, y - 1, rows]
                    below = jnp.where(tile_odd == 1, b, a) if y == lines - 1 else field[m, plane, y + 1, rows]
                    dy.append(below - above)
                    dx.append(slope_x[m, plane, y, rows])
                for e in range(energies):
                    share = [half[mats * e + m] for m in range(mats)]
                    grad_z, grad_y, grad_x = mix(share, dz), mix(share, dy), mix(share, dx)
                    slope_sq = grad_z * grad_z + grad_y * grad_y + grad_x * grad_x
                    root = lax.rsqrt(slope_sq + 1.0)
                    shading = 0.3 + jnp.abs(0.56 * grad_z + 0.336 * grad_y + 0.252 * grad_x) * root
                    hue = [hues[plane, y * groups + group, 4 * e + c] for c in range(4)]
                    taken = keep[e] * (hue[3] * (slope_sq * (root * root)))
                    keep[e] = keep[e] - taken
                    lit = taken * shading
                    for c in range(3):
                        light[e][c] = light[e][c] + lit * hue[c]
                    light[e][3] = light[e][3] + taken
            base = group * (ROWS * pitch) + y
            for e in range(energies):
                for c in range(4):
                    value = light[e][c] * (1.0 / 255.0) if c < 3 else light[e][c]
                    image[pl.ds(base + (c * energies + e) * lines, ROWS, stride=pitch), :] = value
        return 0

    lax.fori_loop(0, groups, chunk, 0)

    def part(pair, _):
        for target, parity in ((kept, depth_odd), (sent, 1 - depth_odd)):
            target[pair] = image[pl.ds((2 * pair + parity) * pitch, kinds), :]
        return 0

    lax.fori_loop(0, blocks // 2, part, 0, unroll=True)


FINE, COARSE, TOP, KNEE = 1500.0, 64.0, 32767.0, 40.0
BEND = TOP - FINE * (KNEE - 1.0)
NOTHING = -32768


def encode(value):
    octave = jnp.log2(jnp.maximum(value, 1e-37))
    code = jnp.maximum(TOP + FINE * (octave + 1.0), BEND + COARSE * (octave + KNEE))
    code = jnp.round(jnp.minimum(code, TOP)).astype(jnp.int32)
    return jnp.where(value > 1e-37, code, NOTHING).astype(jnp.int16)


def decode(code):
    code = code.astype(jnp.int32)
    wide = code.astype(jnp.float32)
    octave = jnp.minimum((wide - TOP) * (1.0 / FINE) - 1.0, (wide - BEND) * (1.0 / COARSE) - KNEE)
    return jnp.where(code > NOTHING, jnp.exp2(octave), 0.0)


def join(per, mine, other, out):
    odd = lax.axis_index("depth") % 2
    for pair in range(mine.shape[0]):
        a, b = mine[pair], other[pair]
        front, back = jnp.where(odd == 0, a, b), jnp.where(odd == 0, b, a)
        clear = 1.0 - front[-per:, :]
        both = [front[i : i + per, :] + clear * back[i : i + per, :] for i in range(0, front.shape[0], per)]
        out[pair] = encode(jnp.concatenate(both, axis=0))


def composite(parts, out):
    bricks, kinds, _ = parts.shape
    energies, channels, lines, _ = out.shape
    per = kinds // channels

    keep = jnp.ones((per, LANES), jnp.float32)
    total = [jnp.zeros((per, LANES), jnp.float32) for _ in range(channels)]
    for brick in range(bricks):
        part = decode(parts[brick])
        for c in range(channels):
            total[c] = total[c] + keep * part[c * per : (c + 1) * per, :]
        keep = keep * (1.0 - part[(channels - 1) * per :, :])
    for c in range(channels):
        for e in range(energies):
            out[e, c] = total[c][e * lines : (e + 1) * lines, :]


def limit(mib):
    return pltpu.CompilerParams(vmem_limit_bytes=mib * 2**20)


def body(density, material_weight, color_table):
    mats, planes, lines, columns = density.shape
    energies = material_weight.shape[0]
    blocks = columns // LANES
    depth = lax.axis_size("depth")
    kinds = 4 * energies * lines
    pairs = blocks // 2
    vmem = pl.BlockSpec(memory_space=pltpu.VMEM)
    real = lambda *shape: jax.ShapeDtypeStruct(shape, jnp.float32)
    short = lambda *shape: jax.ShapeDtypeStruct(shape, density.dtype)

    cells = density.reshape(mats, planes, lines, blocks, LANES)
    rows = [lax.dynamic_index_in_dim(cells, end("tile", high, lines - 1), 2, keepdims=False) for high in (False, True)]
    tile_a = lax.ppermute(rows[0], "tile", partners("tile", 0))
    tile_b = lax.ppermute(rows[1], "tile", partners("tile", 1))

    def send(high, *before):
        return pl.pallas_call(
            functools.partial(plane_to_send, high),
            out_shape=short(mats, lines, blocks, LANES),
            in_specs=[vmem] + [pl.BlockSpec(memory_space=pl.ANY)] * len(before),
            out_specs=vmem,
            compiler_params=limit(2),
            cost_estimate=pl.CostEstimate(flops=1_000_000_000, bytes_accessed=2_000_000, transcendentals=0),
            name="plane_to_send",
        )(cells, *before)

    plane_b = send(True, *rows)
    depth_b = lax.ppermute(plane_b, "depth", partners("depth", 1))
    depth_a = lax.ppermute(send(False, plane_b), "depth", partners("depth", 0))
    hues, field, slope_x, half = pl.pallas_call(
        functools.partial(lookup, planes * depth),
        out_shape=(
            real(planes, lines * blocks // ROWS, 4 * energies, ROWS, LANES),
            real(*cells.shape),
            real(*cells.shape),
            real(energies * mats, ROWS, LANES),
        ),
        in_specs=[vmem] * 3,
        out_specs=(vmem,) * 4,
        scratch_shapes=[
            pltpu.VMEM((energies * mats, ROWS, LANES), jnp.float32),
            pltpu.VMEM((ROWS, LANES), jnp.int32),
            pltpu.VMEM((ROWS, LANES), jnp.int32),
        ],
        compiler_params=limit(8),
        cost_estimate=pl.CostEstimate(flops=4_000_000_000, bytes_accessed=8_000_000, transcendentals=300_000),
        name="lookup",
    )(material_weight, color_table, cells)
    kept, sent = pl.pallas_call(
        shade,
        out_shape=(real(pairs, kinds, LANES),) * 2,
        in_specs=[vmem] * 8,
        out_specs=(vmem, vmem),
        scratch_shapes=[pltpu.VMEM((blocks * (kinds + 1), LANES), jnp.float32)],
        compiler_params=limit(8),
        name="shade",
    )(half, hues, field, slope_x, depth_a, depth_b, tile_a, tile_b)
    other = lax.ppermute(sent, "depth", [(i, i ^ 1) for i in range(depth)])
    joined = pl.pallas_call(
        functools.partial(join, energies * lines),
        out_shape=jax.ShapeDtypeStruct((pairs, kinds, LANES), jnp.int16),
        in_specs=[vmem, vmem],
        out_specs=vmem,
        compiler_params=limit(2),
        name="join",
    )(kept, other)
    same_core = [[2 * i + c for i in range(depth // 2)] for c in range(2)]
    parts = lax.all_to_all(joined, "depth", 0, 0, axis_index_groups=same_core, tiled=True)
    return pl.pallas_call(
        composite,
        out_shape=real(energies, 4, lines, columns // depth),
        in_specs=[vmem],
        out_specs=vmem,
        compiler_params=limit(2),
        name="composite",
    )(parts)


def solution(mesh):
    return jax.shard_map(
        body,
        mesh=mesh,
        in_specs=(P(None, "depth", "tile", None), P(), P()),
        out_specs=P(None, None, "tile", "depth"),
        check_vma=False,
    )
```

```python
import functools
import math

import jax
import jax.numpy as jnp
from jax import lax
from jax.experimental import pallas as pl
from jax.experimental.pallas import tpu as pltpu
from jax.sharding import PartitionSpec as P

LANES = 128
ROWS = 8


AXES = ("depth", "tile")


def partners(axis, start):
    depth, tile = (lax.axis_size(name) for name in AXES)
    pairs = []
    for d in range(depth):
        for t in range(tile):
            place, count = (d, depth) if axis == "depth" else (t, tile)
            other = place + 1 if (place - start) % 2 == 0 else place - 1
            if 0 <= other < count:
                to = (other, t) if axis == "depth" else (d, other)
            else:
                to = (d, t ^ 1) if axis == "depth" else (d ^ 1, t)
            pairs.append((d * tile + t, to[0] * tile + to[1]))
    return pairs


def inside(axis):
    place = lax.axis_index(axis)
    return (place > 0) & (place < lax.axis_size(axis) - 1)


def end(axis, high, last):
    odd = lax.axis_index(axis) % 2
    return last * odd if high else last * (1 - odd)


def mix(weights, parts):
    total = weights[0] * parts[0]
    for weight, part in zip(weights[1:], parts[1:]):
        total = total + weight * part
    return total


def plane_to_send(high, cells, *refs):
    mats, planes, lines, _, _ = cells.shape
    for m in range(mats):
        for y in range(lines):
            refs[-1][m, y] = cells[m, end("depth", high, planes - 1), y]


def rounded(x):
    big = x * 65537.0
    return big - (big - x)


def lookup(depth_total, weight, color_table, cells, hues, field, slope_x, half, power, even, odd):
    mats, planes, lines, blocks, _ = cells.shape
    groups = blocks // ROWS
    energies, channels, bins = color_table.shape

    channel = lax.broadcasted_iota(jnp.int32, (channels, bins), 0)
    words = [jnp.sum(color_table[e] << (8 * channel), axis=0, keepdims=True) for e in range(energies)]
    word = jnp.concatenate(words + words[: ROWS - energies], axis=0)
    place = lax.broadcasted_iota(jnp.int32, (ROWS, LANES), 1)
    twice = (2 * place) & (LANES - 1)
    pick = lambda row, spot: jnp.take_along_axis(row, spot, axis=1, mode="promise_in_bounds")
    for table, spot in ((even, twice), (odd, twice + 1)):
        table[...] = jnp.where(place < LANES // 2, pick(word[:, :LANES], spot), pick(word[:, LANES:], spot))
    for e in range(energies):
        for m in range(mats):
            value = 0.5 * jnp.broadcast_to(weight[e : e + 1, m : m + 1], (ROWS, LANES))
            half[mats * e + m] = value
            power[mats * e + m] = value * (-math.log2(math.e))

    lane = lax.broadcasted_iota(jnp.int32, (blocks, LANES), 1)
    block = lax.broadcasted_iota(jnp.int32, (blocks, LANES), 0)
    zero = jnp.zeros((blocks, LANES), jnp.float32)

    def line(step, _):
        plane, y = step // lines, step % lines
        here = [cells[m, plane, y].astype(jnp.float32) for m in range(mats)]
        for m in range(mats):
            field[m, plane, y] = here[m]
            before = jnp.where(block == 0, zero, pltpu.roll(here[m], 1, 0))
            after = jnp.where(block == blocks - 1, zero, pltpu.roll(here[m], blocks - 1, 0))
            left = pltpu.roll(jnp.where(lane == LANES - 1, before, here[m]), 1, 1)
            right = pltpu.roll(jnp.where(lane == 0, after, here[m]), LANES - 1, 1)
            slope_x[m, plane, y] = right - left
        for group in range(groups):
            middle = [here[m][group * ROWS : (group + 1) * ROWS] for m in range(mats)]
            for e in range(energies):
                fall = jnp.exp2(mix([power[mats * e + m] for m in range(mats)], middle))
                level = 127.5 - 127.5 * fall
                next_even = (level + 0.5).astype(jnp.int32)
                away = jnp.abs(level - next_even.astype(jnp.float32))
                away = away + away
                at_odd, at_even = rounded(away), rounded(1.0 - away)
                word_odd = pick(jnp.broadcast_to(odd[e : e + 1, :], (ROWS, LANES)), level.astype(jnp.int32))
                word_even = pick(jnp.broadcast_to(even[e : e + 1, :], (ROWS, LANES)), next_even)
                level_of = lambda word, c: (lax.shift_right_logical(word, 8 * c) & 255).astype(jnp.float32)
                for c in range(4):
                    hue = at_even * level_of(word_even, c) + at_odd * level_of(word_odd, c)
                    hues[plane, y * groups + group, 4 * e + c] = hue if c < 3 else hue * (6.0 / (255.0 * depth_total))
        return 0

    lax.fori_loop(0, planes * lines, line, 0, unroll=4)


def shade(half, hues, field, slope_x, depth_a, depth_b, tile_a, tile_b, kept, sent, image):
    mats, planes, lines, blocks, _ = field.shape
    energies = half.shape[0] // mats
    groups = blocks // ROWS
    kinds = 4 * energies * lines
    pitch = image.shape[0] // blocks
    tile_odd, depth_odd = lax.axis_index("tile") % 2, lax.axis_index("depth") % 2
    tile_inside, depth_inside = inside("tile"), inside("depth")

    def chunk(group, _):
        rows = pl.ds(pl.multiple_of(group * ROWS, ROWS), ROWS)
        for y in range(lines):
            light = [[jnp.zeros((ROWS, LANES), jnp.float32) for _ in range(4)] for _ in range(energies)]
            keep = [jnp.ones((ROWS, LANES), jnp.float32) for _ in range(energies)]
            near, far = [], []
            for m in range(mats):
                a, b = depth_a[m, y, rows], depth_b[m, y, rows]
                b = jnp.where(depth_inside, b, jnp.zeros_like(b))
                near.append(jnp.where(depth_odd == 1, a, b))
                far.append(jnp.where(depth_odd == 1, b, a))
            for plane in range(planes):
                dx, dy, dz = [], [], []
                for m in range(mats):
                    before = near[m] if plane == 0 else field[m, plane - 1, y, rows]
                    after = far[m] if plane == planes - 1 else field[m, plane + 1, y, rows]
                    dz.append(after - before)
                    a, b = tile_a[m, plane, rows], tile_b[m, plane, rows]
                    b = jnp.where(tile_inside, b, jnp.zeros_like(b))
                    above = jnp.where(tile_odd == 1, a, b) if y == 0 else field[m, plane, y - 1, rows]
                    below = jnp.where(tile_odd == 1, b, a) if y == lines - 1 else field[m, plane, y + 1, rows]
                    dy.append(below - above)
                    dx.append(slope_x[m, plane, y, rows])
                for e in range(energies):
                    share = [half[mats * e + m] for m in range(mats)]
                    grad_z, grad_y, grad_x = mix(share, dz), mix(share, dy), mix(share, dx)
                    slope_sq = grad_z * grad_z + grad_y * grad_y + grad_x * grad_x
                    root = lax.rsqrt(slope_sq + 1.0)
                    shading = 0.3 + jnp.abs(0.56 * grad_z + 0.336 * grad_y + 0.252 * grad_x) * root
                    hue = [hues[plane, y * groups + group, 4 * e + c] for c in range(4)]
                    taken = keep[e] * (hue[3] * (slope_sq * (root * root)))
                    keep[e] = keep[e] - taken
                    lit = taken * shading
                    for c in range(3):
                        light[e][c] = light[e][c] + lit * hue[c]
                    light[e][3] = light[e][3] + taken
            base = group * (ROWS * pitch) + y
            for e in range(energies):
                for c in range(4):
                    value = light[e][c] * (1.0 / 255.0) if c < 3 else light[e][c]
                    image[pl.ds(base + (c * energies + e) * lines, ROWS, stride=pitch), :] = value
        return 0

    lax.fori_loop(0, groups, chunk, 0)

    def part(pair, _):
        for target, parity in ((kept, depth_odd), (sent, 1 - depth_odd)):
            target[pair] = image[pl.ds((2 * pair + parity) * pitch, kinds), :]
        return 0

    lax.fori_loop(0, blocks // 2, part, 0, unroll=True)


FINE, COARSE, TOP, KNEE = 1500.0, 64.0, 32767.0, 40.0
BEND = TOP - FINE * (KNEE - 1.0)
NOTHING = -32768


def encode(value):
    octave = jnp.log2(jnp.maximum(value, 1e-37))
    code = jnp.maximum(TOP + FINE * (octave + 1.0), BEND + COARSE * (octave + KNEE))
    code = jnp.round(jnp.minimum(code, TOP)).astype(jnp.int32)
    return jnp.where(value > 1e-37, code, NOTHING).astype(jnp.int16)


def decode(code):
    code = code.astype(jnp.int32)
    wide = code.astype(jnp.float32)
    octave = jnp.minimum((wide - TOP) * (1.0 / FINE) - 1.0, (wide - BEND) * (1.0 / COARSE) - KNEE)
    return jnp.where(code > NOTHING, jnp.exp2(octave), 0.0)


def join(per, mine, other, out):
    odd = lax.axis_index("depth") % 2
    for pair in range(mine.shape[0]):
        a, b = mine[pair], other[pair]
        front, back = jnp.where(odd == 0, a, b), jnp.where(odd == 0, b, a)
        clear = 1.0 - front[-per:, :]
        both = [front[i : i + per, :] + clear * back[i : i + per, :] for i in range(0, front.shape[0], per)]
        out[pair] = encode(jnp.concatenate(both, axis=0))


def composite(parts, out):
    bricks, kinds, _ = parts.shape
    energies, channels, lines, _ = out.shape
    per = kinds // channels

    keep = jnp.ones((per, LANES), jnp.float32)
    total = [jnp.zeros((per, LANES), jnp.float32) for _ in range(channels)]
    for brick in range(bricks):
        part = decode(parts[brick])
        for c in range(channels):
            total[c] = total[c] + keep * part[c * per : (c + 1) * per, :]
        keep = keep * (1.0 - part[(channels - 1) * per :, :])
    for c in range(channels):
        for e in range(energies):
            out[e, c] = total[c][e * lines : (e + 1) * lines, :]


def limit(mib):
    return pltpu.CompilerParams(vmem_limit_bytes=mib * 2**20)


def body(density, material_weight, color_table):
    mats, planes, lines, columns = density.shape
    energies = material_weight.shape[0]
    blocks = columns // LANES
    depth = lax.axis_size("depth")
    kinds = 4 * energies * lines
    pairs = blocks // 2
    vmem = pl.BlockSpec(memory_space=pltpu.VMEM)
    real = lambda *shape: jax.ShapeDtypeStruct(shape, jnp.float32)
    short = lambda *shape: jax.ShapeDtypeStruct(shape, density.dtype)

    cells = density.reshape(mats, planes, lines, blocks, LANES)
    rows = [lax.dynamic_index_in_dim(cells, end("tile", high, lines - 1), 2, keepdims=False) for high in (False, True)]
    tile_a = lax.ppermute(rows[0], AXES, partners("tile", 0))
    tile_b = lax.ppermute(rows[1], AXES, partners("tile", 1))

    def send(high, *before):
        return pl.pallas_call(
            functools.partial(plane_to_send, high),
            out_shape=short(mats, lines, blocks, LANES),
            in_specs=[vmem] + [pl.BlockSpec(memory_space=pl.ANY)] * len(before),
            out_specs=vmem,
            compiler_params=limit(2),
            cost_estimate=pl.CostEstimate(flops=1_000_000_000, bytes_accessed=2_000_000, transcendentals=0),
            name="plane_to_send",
        )(cells, *before)

    plane_b = send(True, *rows)
    depth_b = lax.ppermute(plane_b, AXES, partners("depth", 1))
    depth_a = lax.ppermute(send(False, plane_b), AXES, partners("depth", 0))
    hues, field, slope_x, half = pl.pallas_call(
        functools.partial(lookup, planes * depth),
        out_shape=(
            real(planes, lines * blocks // ROWS, 4 * energies, ROWS, LANES),
            real(*cells.shape),
            real(*cells.shape),
            real(energies * mats, ROWS, LANES),
        ),
        in_specs=[vmem] * 3,
        out_specs=(vmem,) * 4,
        scratch_shapes=[
            pltpu.VMEM((energies * mats, ROWS, LANES), jnp.float32),
            pltpu.VMEM((ROWS, LANES), jnp.int32),
            pltpu.VMEM((ROWS, LANES), jnp.int32),
        ],
        compiler_params=limit(8),
        cost_estimate=pl.CostEstimate(flops=4_000_000_000, bytes_accessed=8_000_000, transcendentals=300_000),
        name="lookup",
    )(material_weight, color_table, cells)
    kept, sent = pl.pallas_call(
        shade,
        out_shape=(real(pairs, kinds, LANES),) * 2,
        in_specs=[vmem] * 8,
        out_specs=(vmem, vmem),
        scratch_shapes=[pltpu.VMEM((blocks * (kinds + 1), LANES), jnp.float32)],
        compiler_params=limit(8),
        name="shade",
    )(half, hues, field, slope_x, depth_a, depth_b, tile_a, tile_b)
    other = lax.ppermute(sent, "depth", [(i, i ^ 1) for i in range(depth)])
    joined = pl.pallas_call(
        functools.partial(join, energies * lines),
        out_shape=jax.ShapeDtypeStruct((pairs, kinds, LANES), jnp.int16),
        in_specs=[vmem, vmem],
        out_specs=vmem,
        compiler_params=limit(2),
        name="join",
    )(kept, other)
    same_core = [[2 * i + c for i in range(depth // 2)] for c in range(2)]
    parts = lax.all_to_all(joined, "depth", 0, 0, axis_index_groups=same_core, tiled=True)
    return pl.pallas_call(
        composite,
        out_shape=real(energies, 4, lines, columns // depth),
        in_specs=[vmem],
        out_specs=vmem,
        compiler_params=limit(2),
        name="composite",
    )(parts)


def solution(mesh):
    return jax.shard_map(
        body,
        mesh=mesh,
        in_specs=(P(None, "depth", "tile", None), P(), P()),
        out_specs=P(None, None, "tile", "depth"),
        check_vma=False,
    )
```

```python
import functools
import math

import jax
import jax.numpy as jnp
from jax import lax
from jax.experimental import pallas as pl
from jax.experimental.pallas import tpu as pltpu
from jax.sharding import PartitionSpec as P

LANES = 128
ROWS = 8


AXES = ("depth", "tile")


def partners(axis, start):
    depth, tile = (lax.axis_size(name) for name in AXES)
    pairs = []
    for d in range(depth):
        for t in range(tile):
            place, count = (d, depth) if axis == "depth" else (t, tile)
            other = place + 1 if (place - start) % 2 == 0 else place - 1
            if 0 <= other < count:
                to = (other, t) if axis == "depth" else (d, other)
            else:
                to = (d, t ^ 1) if axis == "depth" else (d ^ 1, t)
            pairs.append((d * tile + t, to[0] * tile + to[1]))
    return pairs


def inside(axis):
    place = lax.axis_index(axis)
    return (place > 0) & (place < lax.axis_size(axis) - 1)


def end(axis, high, last):
    odd = lax.axis_index(axis) % 2
    return last * odd if high else last * (1 - odd)


def mix(weights, parts):
    total = weights[0] * parts[0]
    for weight, part in zip(weights[1:], parts[1:]):
        total = total + weight * part
    return total


def plane_to_send(high, cells, *refs):
    mats, planes, lines, _, _ = cells.shape
    for m in range(mats):
        for y in range(lines):
            refs[-1][m, y] = cells[m, end("depth", high, planes - 1), y]


def rounded(x):
    big = x * 65537.0
    return big - (big - x)


def lookup(depth_total, weight, color_table, cells, hues, field, slope_x, half, power, even, odd):
    mats, planes, lines, blocks, _ = cells.shape
    groups = blocks // ROWS
    energies, channels, bins = color_table.shape

    channel = lax.broadcasted_iota(jnp.int32, (channels, bins), 0)
    words = [jnp.sum(color_table[e] << (8 * channel), axis=0, keepdims=True) for e in range(energies)]
    word = jnp.concatenate(words + words[: ROWS - energies], axis=0)
    place = lax.broadcasted_iota(jnp.int32, (ROWS, LANES), 1)
    twice = (2 * place) & (LANES - 1)
    pick = lambda row, spot: jnp.take_along_axis(row, spot, axis=1, mode="promise_in_bounds")
    for table, spot in ((even, twice), (odd, twice + 1)):
        table[...] = jnp.where(place < LANES // 2, pick(word[:, :LANES], spot), pick(word[:, LANES:], spot))
    for e in range(energies):
        for m in range(mats):
            value = 0.5 * jnp.broadcast_to(weight[e : e + 1, m : m + 1], (ROWS, LANES))
            half[mats * e + m] = value
            power[mats * e + m] = value * (-math.log2(math.e))

    lane = lax.broadcasted_iota(jnp.int32, (blocks, LANES), 1)
    block = lax.broadcasted_iota(jnp.int32, (blocks, LANES), 0)
    zero = jnp.zeros((blocks, LANES), jnp.float32)

    def line(step, _):
        plane, y = step // lines, step % lines
        here = [cells[m, plane, y].astype(jnp.float32) for m in range(mats)]
        for m in range(mats):
            field[m, plane, y] = here[m]
            before = jnp.where(block == 0, zero, pltpu.roll(here[m], 1, 0))
            after = jnp.where(block == blocks - 1, zero, pltpu.roll(here[m], blocks - 1, 0))
            left = pltpu.roll(jnp.where(lane == LANES - 1, before, here[m]), 1, 1)
            right = pltpu.roll(jnp.where(lane == 0, after, here[m]), LANES - 1, 1)
            slope_x[m, plane, y] = right - left
        for group in range(groups):
            middle = [here[m][group * ROWS : (group + 1) * ROWS] for m in range(mats)]
            for e in range(energies):
                fall = jnp.exp2(mix([power[mats * e + m] for m in range(mats)], middle))
                level = 127.5 - 127.5 * fall
                next_even = (level + 0.5).astype(jnp.int32)
                away = jnp.abs(level - next_even.astype(jnp.float32))
                away = away + away
                at_odd, at_even = rounded(away), rounded(1.0 - away)
                word_odd = pick(jnp.broadcast_to(odd[e : e + 1, :], (ROWS, LANES)), level.astype(jnp.int32))
                word_even = pick(jnp.broadcast_to(even[e : e + 1, :], (ROWS, LANES)), next_even)
                level_of = lambda word, c: (lax.shift_right_logical(word, 8 * c) & 255).astype(jnp.float32)
                for c in range(4):
                    hue = at_even * level_of(word_even, c) + at_odd * level_of(word_odd, c)
                    hues[plane, y * groups + group, 4 * e + c] = hue if c < 3 else hue * (6.0 / (255.0 * depth_total))
        return 0

    lax.fori_loop(0, planes * lines, line, 0, unroll=4)


def shade(second, half, hues, field, slope_x, depth_a, depth_b, halo, *refs):
    image = refs[-1]
    mats, planes, lines, blocks, _ = field.shape
    energies = half.shape[0] // mats
    groups = blocks // ROWS
    kinds = 4 * energies
    pitch = image.shape[0] // blocks
    tile_odd, depth_odd = lax.axis_index("tile") % 2, lax.axis_index("depth") % 2
    below = tile_odd if second else 1 - tile_odd
    here, beside = below, 1 - below
    sign = jnp.where(below == 1, 1.0, -1.0)
    halo_inside, depth_inside = inside("tile") if second else True, inside("depth")

    def chunk(group, _):
        rows = pl.ds(pl.multiple_of(group * ROWS, ROWS), ROWS)
        light = [[jnp.zeros((ROWS, LANES), jnp.float32) for _ in range(4)] for _ in range(energies)]
        keep = [jnp.ones((ROWS, LANES), jnp.float32) for _ in range(energies)]
        near, far = [], []
        for m in range(mats):
            a, b = depth_a[m, here, rows], depth_b[m, here, rows]
            b = jnp.where(depth_inside, b, jnp.zeros_like(b))
            near.append(jnp.where(depth_odd == 1, a, b))
            far.append(jnp.where(depth_odd == 1, b, a))
        for plane in range(planes):
            dx, dy, dz = [], [], []
            for m in range(mats):
                before = near[m] if plane == 0 else field[m, plane - 1, here, rows]
                after = far[m] if plane == planes - 1 else field[m, plane + 1, here, rows]
                dz.append(after - before)
                outer = halo[m, plane, rows]
                if second:
                    outer = jnp.where(halo_inside, outer, jnp.zeros_like(outer))
                dy.append((outer - field[m, plane, beside, rows]) * sign)
                dx.append(slope_x[m, plane, here, rows])
            for e in range(energies):
                share = [half[mats * e + m] for m in range(mats)]
                grad_z, grad_y, grad_x = mix(share, dz), mix(share, dy), mix(share, dx)
                slope_sq = grad_z * grad_z + grad_y * grad_y + grad_x * grad_x
                root = lax.rsqrt(slope_sq + 1.0)
                shading = 0.3 + jnp.abs(0.56 * grad_z + 0.336 * grad_y + 0.252 * grad_x) * root
                hue = [hues[plane, here * groups + group, 4 * e + c] for c in range(4)]
                taken = keep[e] * (hue[3] * (slope_sq * (root * root)))
                keep[e] = keep[e] - taken
                lit = taken * shading
                for c in range(3):
                    light[e][c] = light[e][c] + lit * hue[c]
                light[e][3] = light[e][3] + taken
        for e in range(energies):
            for c in range(4):
                value = light[e][c] * (1.0 / 255.0) if c < 3 else light[e][c]
                image[pl.ds(group * (ROWS * pitch) + c * energies + e, ROWS, stride=pitch), :] = value
        return 0

    lax.fori_loop(0, groups, chunk, 0)

    if second:
        first_image, kept, sent, _ = refs
        for pair in range(blocks // 2):
            for target, parity in ((kept, depth_odd), (sent, 1 - depth_odd)):
                rows = pl.ds((2 * pair + parity) * pitch, kinds)
                target[pair, :kinds] = first_image[rows, :]
                target[pair, kinds:] = image[rows, :]


FINE, COARSE, TOP, KNEE = 1500.0, 64.0, 32767.0, 40.0
BEND = TOP - FINE * (KNEE - 1.0)
NOTHING = -32768


def encode(value):
    octave = jnp.log2(jnp.maximum(value, 1e-37))
    code = jnp.maximum(TOP + FINE * (octave + 1.0), BEND + COARSE * (octave + KNEE))
    code = jnp.round(jnp.minimum(code, TOP)).astype(jnp.int32)
    return jnp.where(value > 1e-37, code, NOTHING).astype(jnp.int16)


def decode(code):
    code = code.astype(jnp.int32)
    wide = code.astype(jnp.float32)
    octave = jnp.minimum((wide - TOP) * (1.0 / FINE) - 1.0, (wide - BEND) * (1.0 / COARSE) - KNEE)
    return jnp.where(code > NOTHING, jnp.exp2(octave), 0.0)


def opacity(value, per):
    last = value[2 * per :]
    row = lax.broadcasted_iota(jnp.int32, last.shape, 0)
    return jnp.where(row < per, pltpu.roll(last, per, 0), last)


def join(per, mine, other, out):
    odd = lax.axis_index("depth") % 2
    for pair in range(mine.shape[0]):
        a, b = mine[pair], other[pair]
        front, back = jnp.where(odd == 0, a, b), jnp.where(odd == 0, b, a)
        both = []
        for line in range(0, front.shape[0], 4 * per):
            clear = 1.0 - opacity(front[line : line + 4 * per], per)
            for i in range(line, line + 4 * per, 2 * per):
                both.append(front[i : i + 2 * per] + clear * back[i : i + 2 * per])
        out[pair] = encode(jnp.concatenate(both, axis=0))


def composite(parts, out):
    bricks, kinds, _ = parts.shape
    energies, channels, lines, _ = out.shape
    each = channels * energies

    keep = [jnp.ones((2 * energies, LANES), jnp.float32) for _ in range(lines)]
    total = [[jnp.zeros((2 * energies, LANES), jnp.float32) for _ in range(2)] for _ in range(lines)]
    for brick in range(bricks):
        part = decode(parts[brick])
        for k in range(lines):
            line = part[k * each : (k + 1) * each]
            for i in range(2):
                total[k][i] = total[k][i] + keep[k] * line[2 * energies * i : 2 * energies * (i + 1)]
            keep[k] = keep[k] * (1.0 - opacity(line, energies))
    odd = lax.axis_index("tile") % 2
    upper, lower = ([jnp.where(odd == at, *halves) for halves in zip(*total)] for at in (1, 0))
    for c in range(channels):
        for e in range(energies):
            row = (c % 2) * energies + e
            out[e, c] = jnp.concatenate([upper[c // 2][row : row + 1], lower[c // 2][row : row + 1]], axis=0)


def limit(mib):
    return pltpu.CompilerParams(vmem_limit_bytes=mib * 2**20)


def body(density, material_weight, color_table):
    mats, planes, lines, columns = density.shape
    energies = material_weight.shape[0]
    blocks = columns // LANES
    depth = lax.axis_size("depth")
    kinds = 4 * energies * lines
    pairs = blocks // 2
    vmem = pl.BlockSpec(memory_space=pltpu.VMEM)
    real = lambda *shape: jax.ShapeDtypeStruct(shape, jnp.float32)
    short = lambda *shape: jax.ShapeDtypeStruct(shape, density.dtype)

    cells = density.reshape(mats, planes, lines, blocks, LANES)
    rows = [lax.dynamic_index_in_dim(cells, end("tile", high, lines - 1), 2, keepdims=False) for high in (False, True)]
    tile_a = lax.ppermute(rows[0], AXES, partners("tile", 0))
    tile_b = lax.ppermute(rows[1], AXES, partners("tile", 1))

    def send(high, *before):
        return pl.pallas_call(
            functools.partial(plane_to_send, high),
            out_shape=short(mats, lines, blocks, LANES),
            in_specs=[vmem] + [pl.BlockSpec(memory_space=pl.ANY)] * len(before),
            out_specs=vmem,
            compiler_params=limit(2),
            cost_estimate=pl.CostEstimate(flops=1_000_000_000, bytes_accessed=2_000_000, transcendentals=0),
            name="plane_to_send",
        )(cells, *before)

    plane_b = send(True, *rows)
    depth_b = lax.ppermute(plane_b, AXES, partners("depth", 1))
    depth_a = lax.ppermute(send(False, plane_b), AXES, partners("depth", 0))
    hues, field, slope_x, half = pl.pallas_call(
        functools.partial(lookup, planes * depth),
        out_shape=(
            real(planes, lines * blocks // ROWS, 4 * energies, ROWS, LANES),
            real(*cells.shape),
            real(*cells.shape),
            real(energies * mats, ROWS, LANES),
        ),
        in_specs=[vmem] * 3,
        out_specs=(vmem,) * 4,
        scratch_shapes=[
            pltpu.VMEM((energies * mats, ROWS, LANES), jnp.float32),
            pltpu.VMEM((ROWS, LANES), jnp.int32),
            pltpu.VMEM((ROWS, LANES), jnp.int32),
        ],
        compiler_params=limit(8),
        cost_estimate=pl.CostEstimate(flops=4_000_000_000, bytes_accessed=8_000_000, transcendentals=300_000),
        name="lookup",
    )(material_weight, color_table, cells)
    half_kinds = 4 * energies
    tall = real(blocks * (half_kinds + 1), LANES)
    shared = (half, hues, field, slope_x, depth_a, depth_b)
    first_image = pl.pallas_call(
        functools.partial(shade, False),
        out_shape=tall,
        in_specs=[vmem] * 7,
        out_specs=vmem,
        compiler_params=limit(8),
        cost_estimate=pl.CostEstimate(flops=2_000_000_000, bytes_accessed=4_000_000, transcendentals=100_000),
        name="shade_first",
    )(*shared, tile_a)
    kept, sent = pl.pallas_call(
        functools.partial(shade, True),
        out_shape=(real(pairs, kinds, LANES),) * 2,
        in_specs=[vmem] * 8,
        out_specs=(vmem, vmem),
        scratch_shapes=[pltpu.VMEM(tall.shape, jnp.float32)],
        compiler_params=limit(8),
        name="shade_second",
    )(*shared, tile_b, first_image)
    other = lax.ppermute(sent, "depth", [(i, i ^ 1) for i in range(depth)])
    joined = pl.pallas_call(
        functools.partial(join, energies),
        out_shape=jax.ShapeDtypeStruct((pairs, kinds, LANES), jnp.int16),
        in_specs=[vmem, vmem],
        out_specs=vmem,
        compiler_params=limit(2),
        name="join",
    )(kept, other)
    same_core = [[2 * i + c for i in range(depth // 2)] for c in range(2)]
    parts = lax.all_to_all(joined, "depth", 0, 0, axis_index_groups=same_core, tiled=True)
    return pl.pallas_call(
        composite,
        out_shape=real(energies, 4, lines, columns // depth),
        in_specs=[vmem],
        out_specs=vmem,
        compiler_params=limit(2),
        name="composite",
    )(parts)


def solution(mesh):
    return jax.shard_map(
        body,
        mesh=mesh,
        in_specs=(P(None, "depth", "tile", None), P(), P()),
        out_specs=P(None, None, "tile", "depth"),
        check_vma=False,
    )
```

```python
import functools
import math

import jax
import jax.numpy as jnp
from jax import lax
from jax.experimental import pallas as pl
from jax.experimental.pallas import tpu as pltpu
from jax.sharding import PartitionSpec as P

LANES = 128
ROWS = 8


AXES = ("depth", "tile")


def partners(axis, start):
    depth, tile = (lax.axis_size(name) for name in AXES)
    pairs = []
    for d in range(depth):
        for t in range(tile):
            place, count = (d, depth) if axis == "depth" else (t, tile)
            other = place + 1 if (place - start) % 2 == 0 else place - 1
            if 0 <= other < count:
                to = (other, t) if axis == "depth" else (d, other)
            else:
                to = (d, t ^ 1) if axis == "depth" else (d ^ 1, t)
            pairs.append((d * tile + t, to[0] * tile + to[1]))
    return pairs


def inside(axis):
    place = lax.axis_index(axis)
    return (place > 0) & (place < lax.axis_size(axis) - 1)


def end(axis, high, last):
    odd = lax.axis_index(axis) % 2
    return last * odd if high else last * (1 - odd)


def mix(weights, parts):
    total = weights[0] * parts[0]
    for weight, part in zip(weights[1:], parts[1:]):
        total = total + weight * part
    return total


def plane_to_send(high, cells, *refs):
    mats, planes, lines, _, _ = cells.shape
    for m in range(mats):
        for y in range(lines):
            refs[-1][m, y] = cells[m, end("depth", high, planes - 1), y]


def rounded(x):
    big = x * 65537.0
    return big - (big - x)


def lookup(depth_total, weight, color_table, cells, hues, field, slope_x, half, power, even, odd):
    mats, planes, lines, blocks, _ = cells.shape
    groups = blocks // ROWS
    energies, channels, bins = color_table.shape

    channel = lax.broadcasted_iota(jnp.int32, (channels, bins), 0)
    words = [jnp.sum(color_table[e] << (8 * channel), axis=0, keepdims=True) for e in range(energies)]
    word = jnp.concatenate(words + words[: ROWS - energies], axis=0)
    place = lax.broadcasted_iota(jnp.int32, (ROWS, LANES), 1)
    twice = (2 * place) & (LANES - 1)
    pick = lambda row, spot: jnp.take_along_axis(row, spot, axis=1, mode="promise_in_bounds")
    for table, spot in ((even, twice), (odd, twice + 1)):
        table[...] = jnp.where(place < LANES // 2, pick(word[:, :LANES], spot), pick(word[:, LANES:], spot))
    for e in range(energies):
        for m in range(mats):
            value = 0.5 * jnp.broadcast_to(weight[e : e + 1, m : m + 1], (ROWS, LANES))
            half[mats * e + m] = value
            power[mats * e + m] = value * (-math.log2(math.e))

    lane = lax.broadcasted_iota(jnp.int32, (blocks, LANES), 1)
    block = lax.broadcasted_iota(jnp.int32, (blocks, LANES), 0)
    zero = jnp.zeros((blocks, LANES), jnp.float32)

    def line(step, _):
        plane, y = step // lines, step % lines
        here = [cells[m, plane, y].astype(jnp.float32) for m in range(mats)]
        for m in range(mats):
            field[m, plane, y] = here[m]
            before = jnp.where(block == 0, zero, pltpu.roll(here[m], 1, 0))
            after = jnp.where(block == blocks - 1, zero, pltpu.roll(here[m], blocks - 1, 0))
            left = pltpu.roll(jnp.where(lane == LANES - 1, before, here[m]), 1, 1)
            right = pltpu.roll(jnp.where(lane == 0, after, here[m]), LANES - 1, 1)
            slope_x[m, plane, y] = right - left
        for group in range(groups):
            middle = [here[m][group * ROWS : (group + 1) * ROWS] for m in range(mats)]
            for e in range(energies):
                fall = jnp.exp2(mix([power[mats * e + m] for m in range(mats)], middle))
                level = 127.5 - 127.5 * fall
                next_even = (level + 0.5).astype(jnp.int32)
                away = jnp.abs(level - next_even.astype(jnp.float32))
                away = away + away
                at_odd, at_even = rounded(away), rounded(1.0 - away)
                word_odd = pick(jnp.broadcast_to(odd[e : e + 1, :], (ROWS, LANES)), level.astype(jnp.int32))
                word_even = pick(jnp.broadcast_to(even[e : e + 1, :], (ROWS, LANES)), next_even)
                level_of = lambda word, c: (lax.shift_right_logical(word, 8 * c) & 255).astype(jnp.float32)
                for c in range(4):
                    hue = at_even * level_of(word_even, c) + at_odd * level_of(word_odd, c)
                    hues[plane, y * groups + group, 4 * e + c] = hue if c < 3 else hue * (6.0 / (255.0 * depth_total))
        return 0

    lax.fori_loop(0, planes * lines, line, 0, unroll=4)


def shade(second, half, hues, field, slope_x, depth_a, depth_b, halo, *refs):
    image = refs[-1]
    mats, planes, lines, blocks, _ = field.shape
    energies = half.shape[0] // mats
    groups = blocks // ROWS
    kinds = 4 * energies
    pitch = image.shape[0] // blocks
    tile_odd, depth_odd = lax.axis_index("tile") % 2, lax.axis_index("depth") % 2
    below = tile_odd if second else 1 - tile_odd
    here, beside = below, 1 - below
    sign = jnp.where(below == 1, 1.0, -1.0)
    halo_inside, depth_inside = inside("tile") if second else True, inside("depth")

    def chunk(group, _):
        rows = pl.ds(pl.multiple_of(group * ROWS, ROWS), ROWS)
        light = [[jnp.zeros((ROWS, LANES), jnp.float32) for _ in range(4)] for _ in range(energies)]
        keep = [jnp.ones((ROWS, LANES), jnp.float32) for _ in range(energies)]
        near, far = [], []
        for m in range(mats):
            a, b = depth_a[m, here, rows], depth_b[m, here, rows]
            b = jnp.where(depth_inside, b, jnp.zeros_like(b))
            near.append(jnp.where(depth_odd == 1, a, b))
            far.append(jnp.where(depth_odd == 1, b, a))
        for plane in range(planes):
            dx, dy, dz = [], [], []
            for m in range(mats):
                before = near[m] if plane == 0 else field[m, plane - 1, here, rows]
                after = far[m] if plane == planes - 1 else field[m, plane + 1, here, rows]
                dz.append(after - before)
                outer = halo[m, plane, rows]
                if second:
                    outer = jnp.where(halo_inside, outer, jnp.zeros_like(outer))
                dy.append((outer - field[m, plane, beside, rows]) * sign)
                dx.append(slope_x[m, plane, here, rows])
            for e in range(energies):
                share = [half[mats * e + m] for m in range(mats)]
                grad_z, grad_y, grad_x = mix(share, dz), mix(share, dy), mix(share, dx)
                slope_sq = grad_z * grad_z + grad_y * grad_y + grad_x * grad_x
                root = lax.rsqrt(slope_sq + 1.0)
                shading = 0.3 + jnp.abs(0.56 * grad_z + 0.336 * grad_y + 0.252 * grad_x) * root
                hue = [hues[plane, here * groups + group, 4 * e + c] for c in range(4)]
                taken = keep[e] * (hue[3] * (slope_sq * (root * root)))
                keep[e] = keep[e] - taken
                lit = taken * shading
                for c in range(3):
                    light[e][c] = light[e][c] + lit * hue[c]
                light[e][3] = light[e][3] + taken
        for e in range(energies):
            for c in range(4):
                value = light[e][c] * (1.0 / 255.0) if c < 3 else light[e][c]
                image[pl.ds(group * (ROWS * pitch) + c * energies + e, ROWS, stride=pitch), :] = value
        return 0

    lax.fori_loop(0, groups, chunk, 0)

    kept, sent = refs[-3:-1]
    part = pl.ds(kinds if second else 0, kinds)
    for pair in range(blocks // 2):
        for target, parity in ((kept, depth_odd), (sent, 1 - depth_odd)):
            target[pair, part] = image[pl.ds((2 * pair + parity) * pitch, kinds), :]


FINE, COARSE, TOP, KNEE = 1500.0, 64.0, 32767.0, 40.0
BEND = TOP - FINE * (KNEE - 1.0)
NOTHING = -32768


def encode(value):
    octave = jnp.log2(jnp.maximum(value, 1e-37))
    code = jnp.maximum(TOP + FINE * (octave + 1.0), BEND + COARSE * (octave + KNEE))
    code = jnp.round(jnp.minimum(code, TOP)).astype(jnp.int32)
    return jnp.where(value > 1e-37, code, NOTHING).astype(jnp.int16)


def decode(code):
    code = code.astype(jnp.int32)
    wide = code.astype(jnp.float32)
    octave = jnp.minimum((wide - TOP) * (1.0 / FINE) - 1.0, (wide - BEND) * (1.0 / COARSE) - KNEE)
    return jnp.where(code > NOTHING, jnp.exp2(octave), 0.0)


def opacity(value, per):
    last = value[2 * per :]
    row = lax.broadcasted_iota(jnp.int32, last.shape, 0)
    return jnp.where(row < per, pltpu.roll(last, per, 0), last)


def join(per, mine, other, out):
    odd = lax.axis_index("depth") % 2
    for pair in range(mine.shape[0]):
        a, b = mine[pair], other[pair]
        front, back = jnp.where(odd == 0, a, b), jnp.where(odd == 0, b, a)
        both = []
        for line in range(0, front.shape[0], 4 * per):
            clear = 1.0 - opacity(front[line : line + 4 * per], per)
            for i in range(line, line + 4 * per, 2 * per):
                both.append(front[i : i + 2 * per] + clear * back[i : i + 2 * per])
        out[pair] = encode(jnp.concatenate(both, axis=0))


def composite(parts, out):
    bricks, kinds, _ = parts.shape
    energies, channels, lines, _ = out.shape
    each = channels * energies

    keep = [jnp.ones((2 * energies, LANES), jnp.float32) for _ in range(lines)]
    total = [[jnp.zeros((2 * energies, LANES), jnp.float32) for _ in range(2)] for _ in range(lines)]
    for brick in range(bricks):
        part = decode(parts[brick])
        for k in range(lines):
            line = part[k * each : (k + 1) * each]
            for i in range(2):
                total[k][i] = total[k][i] + keep[k] * line[2 * energies * i : 2 * energies * (i + 1)]
            keep[k] = keep[k] * (1.0 - opacity(line, energies))
    odd = lax.axis_index("tile") % 2
    upper, lower = ([jnp.where(odd == at, *halves) for halves in zip(*total)] for at in (1, 0))
    for c in range(channels):
        for e in range(energies):
            row = (c % 2) * energies + e
            out[e, c] = jnp.concatenate([upper[c // 2][row : row + 1], lower[c // 2][row : row + 1]], axis=0)


def limit(mib):
    return pltpu.CompilerParams(vmem_limit_bytes=mib * 2**20)


def body(density, material_weight, color_table):
    mats, planes, lines, columns = density.shape
    energies = material_weight.shape[0]
    blocks = columns // LANES
    depth = lax.axis_size("depth")
    kinds = 4 * energies * lines
    pairs = blocks // 2
    vmem = pl.BlockSpec(memory_space=pltpu.VMEM)
    real = lambda *shape: jax.ShapeDtypeStruct(shape, jnp.float32)
    short = lambda *shape: jax.ShapeDtypeStruct(shape, density.dtype)

    cells = density.reshape(mats, planes, lines, blocks, LANES)
    rows = [lax.dynamic_index_in_dim(cells, end("tile", high, lines - 1), 2, keepdims=False) for high in (False, True)]
    tile_a = lax.ppermute(rows[0], AXES, partners("tile", 0))
    tile_b = lax.ppermute(rows[1], AXES, partners("tile", 1))

    def send(high, *before):
        return pl.pallas_call(
            functools.partial(plane_to_send, high),
            out_shape=short(mats, lines, blocks, LANES),
            in_specs=[vmem] + [pl.BlockSpec(memory_space=pl.ANY)] * len(before),
            out_specs=vmem,
            compiler_params=limit(2),
            cost_estimate=pl.CostEstimate(flops=1_000_000_000, bytes_accessed=2_000_000, transcendentals=0),
            name="plane_to_send",
        )(cells, *before)

    plane_b = send(True, *rows)
    depth_b = lax.ppermute(plane_b, AXES, partners("depth", 1))
    depth_a = lax.ppermute(send(False, plane_b), AXES, partners("depth", 0))
    hues, field, slope_x, half = pl.pallas_call(
        functools.partial(lookup, planes * depth),
        out_shape=(
            real(planes, lines * blocks // ROWS, 4 * energies, ROWS, LANES),
            real(*cells.shape),
            real(*cells.shape),
            real(energies * mats, ROWS, LANES),
        ),
        in_specs=[vmem] * 3,
        out_specs=(vmem,) * 4,
        scratch_shapes=[
            pltpu.VMEM((energies * mats, ROWS, LANES), jnp.float32),
            pltpu.VMEM((ROWS, LANES), jnp.int32),
            pltpu.VMEM((ROWS, LANES), jnp.int32),
        ],
        compiler_params=limit(8),
        cost_estimate=pl.CostEstimate(flops=4_000_000_000, bytes_accessed=8_000_000, transcendentals=300_000),
        name="lookup",
    )(material_weight, color_table, cells)
    half_kinds = 4 * energies
    tall = real(blocks * (half_kinds + 1) + 3 * ROWS, LANES)
    shared = (half, hues, field, slope_x, depth_a, depth_b)
    kept = sent = None
    for second, halo in ((False, tile_a), (True, tile_b)):
        filled = (kept, sent) if second else ()
        kept, sent = pl.pallas_call(
            functools.partial(shade, second),
            out_shape=(real(pairs, kinds, LANES),) * 2,
            in_specs=[vmem] * (7 + len(filled)),
            out_specs=(vmem, vmem),
            scratch_shapes=[pltpu.VMEM(tall.shape, jnp.float32)],
            input_output_aliases={7: 0, 8: 1} if second else {},
            compiler_params=limit(8),
            cost_estimate=pl.CostEstimate(flops=2_000_000_000, bytes_accessed=4_000_000, transcendentals=100_000),
            name="shade_second" if second else "shade_first",
        )(*shared, halo, *filled)
    other = lax.ppermute(sent, "depth", [(i, i ^ 1) for i in range(depth)])
    joined = pl.pallas_call(
        functools.partial(join, energies),
        out_shape=jax.ShapeDtypeStruct((pairs, kinds, LANES), jnp.int16),
        in_specs=[vmem, vmem],
        out_specs=vmem,
        compiler_params=limit(2),
        name="join",
    )(kept, other)
    same_core = [[2 * i + c for i in range(depth // 2)] for c in range(2)]
    parts = lax.all_to_all(joined, "depth", 0, 0, axis_index_groups=same_core, tiled=True)
    return pl.pallas_call(
        composite,
        out_shape=real(energies, 4, lines, columns // depth),
        in_specs=[vmem],
        out_specs=vmem,
        compiler_params=limit(2),
        name="composite",
    )(parts)


def solution(mesh):
    return jax.shard_map(
        body,
        mesh=mesh,
        in_specs=(P(None, "depth", "tile", None), P(), P()),
        out_specs=P(None, None, "tile", "depth"),
        check_vma=False,
    )
```

```python
import functools
import math

import jax
import jax.numpy as jnp
from jax import lax
from jax.experimental import pallas as pl
from jax.experimental.pallas import tpu as pltpu
from jax.sharding import PartitionSpec as P

LANES = 128
ROWS = 8


AXES = ("depth", "tile")


def partners(axis, start):
    depth, tile = (lax.axis_size(name) for name in AXES)
    pairs = []
    for d in range(depth):
        for t in range(tile):
            place, count = (d, depth) if axis == "depth" else (t, tile)
            other = place + 1 if (place - start) % 2 == 0 else place - 1
            if 0 <= other < count:
                to = (other, t) if axis == "depth" else (d, other)
            else:
                to = (d, t ^ 1) if axis == "depth" else (d ^ 1, t)
            pairs.append((d * tile + t, to[0] * tile + to[1]))
    return pairs


def inside(axis):
    place = lax.axis_index(axis)
    return (place > 0) & (place < lax.axis_size(axis) - 1)


def end(axis, high, last):
    odd = lax.axis_index(axis) % 2
    return last * odd if high else last * (1 - odd)


def mix(weights, parts):
    total = weights[0] * parts[0]
    for weight, part in zip(weights[1:], parts[1:]):
        total = total + weight * part
    return total


def plane_to_send(high, cells, *refs):
    mats, planes, lines, _, _ = cells.shape
    for m in range(mats):
        for y in range(lines):
            refs[-1][m, y] = cells[m, end("depth", high, planes - 1), y]


def rounded(x):
    big = x * 65537.0
    return big - (big - x)


def lookup(depth_total, weight, color_table, cells, hues, field, slope_x, half, power, even, odd):
    mats, planes, lines, blocks, _ = cells.shape
    groups = blocks // ROWS
    energies, channels, bins = color_table.shape

    channel = lax.broadcasted_iota(jnp.int32, (channels, bins), 0)
    words = [jnp.sum(color_table[e] << (8 * channel), axis=0, keepdims=True) for e in range(energies)]
    word = jnp.concatenate(words + words[: ROWS - energies], axis=0)
    place = lax.broadcasted_iota(jnp.int32, (ROWS, LANES), 1)
    twice = (2 * place) & (LANES - 1)
    pick = lambda row, spot: jnp.take_along_axis(row, spot, axis=1, mode="promise_in_bounds")
    for table, spot in ((even, twice), (odd, twice + 1)):
        table[...] = jnp.where(place < LANES // 2, pick(word[:, :LANES], spot), pick(word[:, LANES:], spot))
    for e in range(energies):
        for m in range(mats):
            value = 0.5 * jnp.broadcast_to(weight[e : e + 1, m : m + 1], (ROWS, LANES))
            half[mats * e + m] = value
            power[mats * e + m] = value * (-math.log2(math.e))

    lane = lax.broadcasted_iota(jnp.int32, (blocks, LANES), 1)
    block = lax.broadcasted_iota(jnp.int32, (blocks, LANES), 0)
    zero = jnp.zeros((blocks, LANES), jnp.float32)

    def line(step, _):
        plane, y = step // lines, step % lines
        here = [cells[m, plane, y].astype(jnp.float32) for m in range(mats)]
        for m in range(mats):
            field[m, plane, y] = here[m]
            before = jnp.where(block == 0, zero, pltpu.roll(here[m], 1, 0))
            after = jnp.where(block == blocks - 1, zero, pltpu.roll(here[m], blocks - 1, 0))
            left = pltpu.roll(jnp.where(lane == LANES - 1, before, here[m]), 1, 1)
            right = pltpu.roll(jnp.where(lane == 0, after, here[m]), LANES - 1, 1)
            slope_x[m, plane, y] = right - left
        for group in range(groups):
            middle = [here[m][group * ROWS : (group + 1) * ROWS] for m in range(mats)]
            for e in range(energies):
                fall = jnp.exp2(mix([power[mats * e + m] for m in range(mats)], middle))
                level = 127.5 - 127.5 * fall
                next_even = (level + 0.5).astype(jnp.int32)
                away = jnp.abs(level - next_even.astype(jnp.float32))
                away = away + away
                at_odd, at_even = rounded(away), rounded(1.0 - away)
                word_odd = pick(jnp.broadcast_to(odd[e : e + 1, :], (ROWS, LANES)), level.astype(jnp.int32))
                word_even = pick(jnp.broadcast_to(even[e : e + 1, :], (ROWS, LANES)), next_even)
                shift = lambda word, c: lax.shift_right_logical(word, 8 * c) if c else word
                level_of = lambda word, c: (shift(word, c) & 255 if c < 3 else shift(word, c)).astype(jnp.float32)
                for c in range(4):
                    hue = at_even * level_of(word_even, c) + at_odd * level_of(word_odd, c)
                    hues[plane, y * groups + group, 4 * e + c] = hue if c < 3 else hue * (6.0 / (255.0 * depth_total))
        return 0

    lax.fori_loop(0, planes * lines, line, 0, unroll=8)


def shade(second, half, hues, field, slope_x, depth_a, depth_b, halo, *refs):
    image = refs[-1]
    mats, planes, lines, blocks, _ = field.shape
    energies = half.shape[0] // mats
    groups = blocks // ROWS
    kinds = 4 * energies
    pitch = image.shape[0] // blocks
    tile_odd, depth_odd = lax.axis_index("tile") % 2, lax.axis_index("depth") % 2
    below = tile_odd if second else 1 - tile_odd
    here, beside = below, 1 - below
    sign = jnp.where(below == 1, 1.0, -1.0)
    halo_inside, depth_inside = inside("tile") if second else True, inside("depth")

    def chunk(group, _):
        rows = pl.ds(pl.multiple_of(group * ROWS, ROWS), ROWS)
        light = [[jnp.zeros((ROWS, LANES), jnp.float32) for _ in range(4)] for _ in range(energies)]
        keep = [jnp.ones((ROWS, LANES), jnp.float32) for _ in range(energies)]
        near, far = [], []
        for m in range(mats):
            a, b = depth_a[m, here, rows], depth_b[m, here, rows]
            b = jnp.where(depth_inside, b, jnp.zeros_like(b))
            near.append(jnp.where(depth_odd == 1, a, b))
            far.append(jnp.where(depth_odd == 1, b, a))
        for plane in range(planes):
            dx, dy, dz = [], [], []
            for m in range(mats):
                before = near[m] if plane == 0 else field[m, plane - 1, here, rows]
                after = far[m] if plane == planes - 1 else field[m, plane + 1, here, rows]
                dz.append(after - before)
                outer = halo[m, plane, rows]
                if second:
                    outer = jnp.where(halo_inside, outer, jnp.zeros_like(outer))
                dy.append((outer - field[m, plane, beside, rows]) * sign)
                dx.append(slope_x[m, plane, here, rows])
            for e in range(energies):
                share = [half[mats * e + m] for m in range(mats)]
                grad_z, grad_y, grad_x = mix(share, dz), mix(share, dy), mix(share, dx)
                slope_sq = grad_z * grad_z + grad_y * grad_y + grad_x * grad_x
                root = lax.rsqrt(slope_sq + 1.0)
                shading = 0.3 + jnp.abs(0.56 * grad_z + 0.336 * grad_y + 0.252 * grad_x) * root
                hue = [hues[plane, here * groups + group, 4 * e + c] for c in range(4)]
                taken = keep[e] * (hue[3] * (slope_sq * (root * root)))
                keep[e] = keep[e] - taken
                lit = taken * shading
                for c in range(3):
                    light[e][c] = light[e][c] + lit * hue[c]
                light[e][3] = light[e][3] + taken
        for e in range(energies):
            for c in range(4):
                value = light[e][c] * (1.0 / 255.0) if c < 3 else light[e][c]
                image[pl.ds(group * (ROWS * pitch) + c * energies + e, ROWS, stride=pitch), :] = value
        return 0

    lax.fori_loop(0, groups, chunk, 0)

    kept, sent = refs[-3:-1]
    part = pl.ds(kinds if second else 0, kinds)
    for pair in range(blocks // 2):
        for target, parity in ((kept, depth_odd), (sent, 1 - depth_odd)):
            target[pair, part] = image[pl.ds((2 * pair + parity) * pitch, kinds), :]


FINE, COARSE, TOP, KNEE = 1500.0, 64.0, 32767.0, 40.0
BEND = TOP - FINE * (KNEE - 1.0)
NOTHING = -32768


def encode(value):
    octave = jnp.log2(jnp.maximum(value, 1e-37))
    code = jnp.maximum(TOP + FINE * (octave + 1.0), BEND + COARSE * (octave + KNEE))
    code = jnp.round(jnp.minimum(code, TOP)).astype(jnp.int32)
    return jnp.where(value > 1e-37, code, NOTHING).astype(jnp.int16)


def decode(code):
    code = code.astype(jnp.int32)
    wide = code.astype(jnp.float32)
    octave = jnp.minimum((wide - TOP) * (1.0 / FINE) - 1.0, (wide - BEND) * (1.0 / COARSE) - KNEE)
    return jnp.where(code > NOTHING, jnp.exp2(octave), 0.0)


def opacity(value, per):
    last = value[2 * per :]
    row = lax.broadcasted_iota(jnp.int32, last.shape, 0)
    return jnp.where(row < per, pltpu.roll(last, per, 0), last)


def join(per, mine, other, out):
    odd = lax.axis_index("depth") % 2
    for pair in range(mine.shape[0]):
        a, b = mine[pair], other[pair]
        front, back = jnp.where(odd == 0, a, b), jnp.where(odd == 0, b, a)
        both = []
        for line in range(0, front.shape[0], 4 * per):
            clear = 1.0 - opacity(front[line : line + 4 * per], per)
            for i in range(line, line + 4 * per, 2 * per):
                both.append(front[i : i + 2 * per] + clear * back[i : i + 2 * per])
        out[pair] = encode(jnp.concatenate(both, axis=0))


def composite(parts, out):
    bricks, kinds, _ = parts.shape
    energies, channels, lines, _ = out.shape
    each = channels * energies

    keep = [jnp.ones((2 * energies, LANES), jnp.float32) for _ in range(lines)]
    total = [[jnp.zeros((2 * energies, LANES), jnp.float32) for _ in range(2)] for _ in range(lines)]
    for brick in range(bricks):
        part = decode(parts[brick])
        for k in range(lines):
            line = part[k * each : (k + 1) * each]
            for i in range(2):
                total[k][i] = total[k][i] + keep[k] * line[2 * energies * i : 2 * energies * (i + 1)]
            keep[k] = keep[k] * (1.0 - opacity(line, energies))
    odd = lax.axis_index("tile") % 2
    upper, lower = ([jnp.where(odd == at, *halves) for halves in zip(*total)] for at in (1, 0))
    for c in range(channels):
        for e in range(energies):
            row = (c % 2) * energies + e
            out[e, c] = jnp.concatenate([upper[c // 2][row : row + 1], lower[c // 2][row : row + 1]], axis=0)


def limit(mib):
    return pltpu.CompilerParams(vmem_limit_bytes=mib * 2**20)


def body(density, material_weight, color_table):
    mats, planes, lines, columns = density.shape
    energies = material_weight.shape[0]
    blocks = columns // LANES
    depth = lax.axis_size("depth")
    kinds = 4 * energies * lines
    pairs = blocks // 2
    vmem = pl.BlockSpec(memory_space=pltpu.VMEM)
    real = lambda *shape: jax.ShapeDtypeStruct(shape, jnp.float32)
    short = lambda *shape: jax.ShapeDtypeStruct(shape, density.dtype)

    cells = density.reshape(mats, planes, lines, blocks, LANES)
    rows = [lax.dynamic_index_in_dim(cells, end("tile", high, lines - 1), 2, keepdims=False) for high in (False, True)]
    tile_a = lax.ppermute(rows[0], AXES, partners("tile", 0))
    tile_b = lax.ppermute(rows[1], AXES, partners("tile", 1))

    def send(high, *before):
        return pl.pallas_call(
            functools.partial(plane_to_send, high),
            out_shape=short(mats, lines, blocks, LANES),
            in_specs=[vmem] + [pl.BlockSpec(memory_space=pl.ANY)] * len(before),
            out_specs=vmem,
            compiler_params=limit(2),
            cost_estimate=pl.CostEstimate(flops=1_000_000_000, bytes_accessed=2_000_000, transcendentals=0),
            name="plane_to_send",
        )(cells, *before)

    plane_b = send(True, *rows)
    depth_b = lax.ppermute(plane_b, AXES, partners("depth", 1))
    depth_a = lax.ppermute(send(False, plane_b), AXES, partners("depth", 0))
    hues, field, slope_x, half = pl.pallas_call(
        functools.partial(lookup, planes * depth),
        out_shape=(
            real(planes, lines * blocks // ROWS, 4 * energies, ROWS, LANES),
            real(*cells.shape),
            real(*cells.shape),
            real(energies * mats, ROWS, LANES),
        ),
        in_specs=[vmem] * 3,
        out_specs=(vmem,) * 4,
        scratch_shapes=[
            pltpu.VMEM((energies * mats, ROWS, LANES), jnp.float32),
            pltpu.VMEM((ROWS, LANES), jnp.int32),
            pltpu.VMEM((ROWS, LANES), jnp.int32),
        ],
        compiler_params=limit(8),
        cost_estimate=pl.CostEstimate(flops=4_000_000_000, bytes_accessed=8_000_000, transcendentals=300_000),
        name="lookup",
    )(material_weight, color_table, cells)
    half_kinds = 4 * energies
    tall = real(blocks * (half_kinds + 1) + 3 * ROWS, LANES)
    shared = (half, hues, field, slope_x, depth_a, depth_b)
    kept = sent = None
    for second, halo in ((False, tile_a), (True, tile_b)):
        filled = (kept, sent) if second else ()
        kept, sent = pl.pallas_call(
            functools.partial(shade, second),
            out_shape=(real(pairs, kinds, LANES),) * 2,
            in_specs=[vmem] * (7 + len(filled)),
            out_specs=(vmem, vmem),
            scratch_shapes=[pltpu.VMEM(tall.shape, jnp.float32)],
            input_output_aliases={7: 0, 8: 1} if second else {},
            compiler_params=limit(8),
            cost_estimate=pl.CostEstimate(flops=2_000_000_000, bytes_accessed=4_000_000, transcendentals=100_000),
            name="shade_second" if second else "shade_first",
        )(*shared, halo, *filled)
    other = lax.ppermute(sent, "depth", [(i, i ^ 1) for i in range(depth)])
    joined = pl.pallas_call(
        functools.partial(join, energies),
        out_shape=jax.ShapeDtypeStruct((pairs, kinds, LANES), jnp.int16),
        in_specs=[vmem, vmem],
        out_specs=vmem,
        compiler_params=limit(2),
        name="join",
    )(kept, other)
    same_core = [[2 * i + c for i in range(depth // 2)] for c in range(2)]
    parts = lax.all_to_all(joined, "depth", 0, 0, axis_index_groups=same_core, tiled=True)
    return pl.pallas_call(
        composite,
        out_shape=real(energies, 4, lines, columns // depth),
        in_specs=[vmem],
        out_specs=vmem,
        compiler_params=limit(2),
        name="composite",
    )(parts)


def solution(mesh):
    return jax.shard_map(
        body,
        mesh=mesh,
        in_specs=(P(None, "depth", "tile", None), P(), P()),
        out_specs=P(None, None, "tile", "depth"),
        check_vma=False,
    )
```

```python
import functools
import math

import jax
import jax.numpy as jnp
from jax import lax
from jax.experimental import pallas as pl
from jax.experimental.pallas import tpu as pltpu
from jax.sharding import PartitionSpec as P

LANES = 128
ROWS = 8


AXES = ("depth", "tile")


def partners(axis, start):
    depth, tile = (lax.axis_size(name) for name in AXES)
    pairs = []
    for d in range(depth):
        for t in range(tile):
            place, count = (d, depth) if axis == "depth" else (t, tile)
            other = place + 1 if (place - start) % 2 == 0 else place - 1
            if 0 <= other < count:
                to = (other, t) if axis == "depth" else (d, other)
            else:
                to = (d, t ^ 1) if axis == "depth" else (d ^ 1, t)
            pairs.append((d * tile + t, to[0] * tile + to[1]))
    return pairs


def inside(axis):
    place = lax.axis_index(axis)
    return (place > 0) & (place < lax.axis_size(axis) - 1)


def end(axis, high, last):
    odd = lax.axis_index(axis) % 2
    return last * odd if high else last * (1 - odd)


def mix(weights, parts):
    total = weights[0] * parts[0]
    for weight, part in zip(weights[1:], parts[1:]):
        total = total + weight * part
    return total


def plane_to_send(high, cells, *refs):
    mats, planes, lines, _, _ = cells.shape
    for m in range(mats):
        for y in range(lines):
            refs[-1][m, y] = cells[m, end("depth", high, planes - 1), y]


def rounded(x):
    big = x * 65537.0
    return big - (big - x)


def lookup(depth_total, weight, color_table, cells, hues, field, slope_x, half, power, even, odd):
    mats, planes, lines, blocks, _ = cells.shape
    groups = blocks // ROWS
    energies, channels, bins = color_table.shape

    channel = lax.broadcasted_iota(jnp.int32, (channels, bins), 0)
    words = [jnp.sum(color_table[e] << (8 * channel), axis=0, keepdims=True) for e in range(energies)]
    word = jnp.concatenate(words + words[: ROWS - energies], axis=0)
    place = lax.broadcasted_iota(jnp.int32, (ROWS, LANES), 1)
    twice = (2 * place) & (LANES - 1)
    pick = lambda row, spot: jnp.take_along_axis(row, spot, axis=1, mode="promise_in_bounds")
    for table, spot in ((even, twice), (odd, twice + 1)):
        table[...] = jnp.where(place < LANES // 2, pick(word[:, :LANES], spot), pick(word[:, LANES:], spot))
    for e in range(energies):
        for m in range(mats):
            value = 0.5 * jnp.broadcast_to(weight[e : e + 1, m : m + 1], (ROWS, LANES))
            half[mats * e + m] = value
            power[mats * e + m] = value * (-math.log2(math.e))

    lane = lax.broadcasted_iota(jnp.int32, (blocks, LANES), 1)
    block = lax.broadcasted_iota(jnp.int32, (blocks, LANES), 0)
    zero = jnp.zeros((blocks, LANES), jnp.float32)

    def line(step, _):
        plane, y = step // lines, step % lines
        here = [cells[m, plane, y].astype(jnp.float32) for m in range(mats)]
        for m in range(mats):
            field[m, plane, y] = here[m]
            before = jnp.where(block == 0, zero, pltpu.roll(here[m], 1, 0))
            after = jnp.where(block == blocks - 1, zero, pltpu.roll(here[m], blocks - 1, 0))
            left = pltpu.roll(jnp.where(lane == LANES - 1, before, here[m]), 1, 1)
            right = pltpu.roll(jnp.where(lane == 0, after, here[m]), LANES - 1, 1)
            slope_x[m, plane, y] = right - left
        for group in range(groups):
            middle = [here[m][group * ROWS : (group + 1) * ROWS] for m in range(mats)]
            for e in range(energies):
                fall = jnp.exp2(mix([power[mats * e + m] for m in range(mats)], middle))
                level = 127.5 - 127.5 * fall
                next_even = (level + 0.5).astype(jnp.int32)
                away = jnp.abs(level - next_even.astype(jnp.float32))
                away = away + away
                at_odd, at_even = rounded(away), rounded(1.0 - away)
                word_odd = pick(jnp.broadcast_to(odd[e : e + 1, :], (ROWS, LANES)), level.astype(jnp.int32))
                word_even = pick(jnp.broadcast_to(even[e : e + 1, :], (ROWS, LANES)), next_even)
                shift = lambda word, c: lax.shift_right_logical(word, 8 * c) if c else word
                level_of = lambda word, c: (shift(word, c) & 255 if c < 3 else shift(word, c)).astype(jnp.float32)
                for c in range(4):
                    hue = at_even * level_of(word_even, c) + at_odd * level_of(word_odd, c)
                    hues[plane, y * groups + group, 4 * e + c] = hue if c < 3 else hue * (6.0 / (255.0 * depth_total))
        return 0

    lax.fori_loop(0, planes * lines, line, 0, unroll=8)


def shade(second, half, hues, field, slope_x, depth_a, depth_b, halo, *refs):
    image = refs[-1]
    mats, planes, lines, blocks, _ = field.shape
    energies = half.shape[0] // mats
    groups = blocks // ROWS
    kinds = 4 * energies
    pitch = image.shape[0] // blocks
    tile_odd, depth_odd = lax.axis_index("tile") % 2, lax.axis_index("depth") % 2
    below = tile_odd if second else 1 - tile_odd
    here, beside = below, 1 - below
    sign = jnp.where(below == 1, 1.0, -1.0)
    halo_inside, depth_inside = inside("tile") if second else True, inside("depth")

    def chunk(group, _):
        rows = pl.ds(pl.multiple_of(group * ROWS, ROWS), ROWS)
        light = [[jnp.zeros((ROWS, LANES), jnp.float32) for _ in range(4)] for _ in range(energies)]
        keep = [jnp.ones((ROWS, LANES), jnp.float32) for _ in range(energies)]
        near, far = [], []
        for m in range(mats):
            a, b = depth_a[m, here, rows], depth_b[m, here, rows]
            b = jnp.where(depth_inside, b, jnp.zeros_like(b))
            near.append(jnp.where(depth_odd == 1, a, b))
            far.append(jnp.where(depth_odd == 1, b, a))
        for plane in range(planes):
            dx, dy, dz = [], [], []
            for m in range(mats):
                before = near[m] if plane == 0 else field[m, plane - 1, here, rows]
                after = far[m] if plane == planes - 1 else field[m, plane + 1, here, rows]
                dz.append(after - before)
                outer = halo[m, plane, rows]
                if second:
                    outer = jnp.where(halo_inside, outer, jnp.zeros_like(outer))
                dy.append((outer - field[m, plane, beside, rows]) * sign)
                dx.append(slope_x[m, plane, here, rows])
            for e in range(energies):
                share = [half[mats * e + m] for m in range(mats)]
                grad_z, grad_y, grad_x = mix(share, dz), mix(share, dy), mix(share, dx)
                slope_sq = grad_z * grad_z + grad_y * grad_y + grad_x * grad_x
                root = lax.rsqrt(slope_sq + 1.0)
                shading = 0.3 + jnp.abs(0.56 * grad_z + 0.336 * grad_y + 0.252 * grad_x) * root
                hue = [hues[plane, here * groups + group, 4 * e + c] for c in range(4)]
                taken = keep[e] * (hue[3] * (slope_sq * (root * root)))
                keep[e] = keep[e] - taken
                lit = taken * shading
                for c in range(3):
                    light[e][c] = light[e][c] + lit * hue[c]
                light[e][3] = light[e][3] + taken
        for e in range(energies):
            for c in range(4):
                value = light[e][c] * (1.0 / 255.0) if c < 3 else light[e][c]
                image[pl.ds(group * (ROWS * pitch) + c * energies + e, ROWS, stride=pitch), :] = value
        return 0

    lax.fori_loop(0, groups, chunk, 0, unroll=2)

    kept, sent = refs[-3:-1]
    part = pl.ds(kinds if second else 0, kinds)
    for pair in range(blocks // 2):
        for target, parity in ((kept, depth_odd), (sent, 1 - depth_odd)):
            target[pair, part] = image[pl.ds((2 * pair + parity) * pitch, kinds), :]


FINE, COARSE, TOP, KNEE = 1500.0, 64.0, 32767.0, 40.0
BEND = TOP - FINE * (KNEE - 1.0)
NOTHING = -32768


def encode(value):
    octave = jnp.log2(jnp.maximum(value, 1e-37))
    code = jnp.maximum(TOP + FINE * (octave + 1.0), BEND + COARSE * (octave + KNEE))
    code = jnp.round(jnp.minimum(code, TOP)).astype(jnp.int32)
    return jnp.where(value > 1e-37, code, NOTHING).astype(jnp.int16)


def decode(code):
    code = code.astype(jnp.int32)
    wide = code.astype(jnp.float32)
    octave = jnp.minimum((wide - TOP) * (1.0 / FINE) - 1.0, (wide - BEND) * (1.0 / COARSE) - KNEE)
    return jnp.where(code > NOTHING, jnp.exp2(octave), 0.0)


def opacity(value, per):
    last = value[2 * per :]
    row = lax.broadcasted_iota(jnp.int32, last.shape, 0)
    return jnp.where(row < per, pltpu.roll(last, per, 0), last)


def join(per, mine, other, out):
    odd = lax.axis_index("depth") % 2
    for pair in range(mine.shape[0]):
        a, b = mine[pair], other[pair]
        front, back = jnp.where(odd == 0, a, b), jnp.where(odd == 0, b, a)
        both = []
        for line in range(0, front.shape[0], 4 * per):
            clear = 1.0 - opacity(front[line : line + 4 * per], per)
            for i in range(line, line + 4 * per, 2 * per):
                both.append(front[i : i + 2 * per] + clear * back[i : i + 2 * per])
        out[pair] = encode(jnp.concatenate(both, axis=0))


def composite(parts, out):
    bricks, kinds, _ = parts.shape
    energies, channels, lines, _ = out.shape
    each = channels * energies

    keep = [jnp.ones((2 * energies, LANES), jnp.float32) for _ in range(lines)]
    total = [[jnp.zeros((2 * energies, LANES), jnp.float32) for _ in range(2)] for _ in range(lines)]
    for brick in range(bricks):
        part = decode(parts[brick])
        for k in range(lines):
            line = part[k * each : (k + 1) * each]
            for i in range(2):
                total[k][i] = total[k][i] + keep[k] * line[2 * energies * i : 2 * energies * (i + 1)]
            keep[k] = keep[k] * (1.0 - opacity(line, energies))
    odd = lax.axis_index("tile") % 2
    upper, lower = ([jnp.where(odd == at, *halves) for halves in zip(*total)] for at in (1, 0))
    for c in range(channels):
        for e in range(energies):
            row = (c % 2) * energies + e
            out[e, c] = jnp.concatenate([upper[c // 2][row : row + 1], lower[c // 2][row : row + 1]], axis=0)


def limit(mib):
    return pltpu.CompilerParams(vmem_limit_bytes=mib * 2**20)


def body(density, material_weight, color_table):
    mats, planes, lines, columns = density.shape
    energies = material_weight.shape[0]
    blocks = columns // LANES
    depth = lax.axis_size("depth")
    kinds = 4 * energies * lines
    pairs = blocks // 2
    vmem = pl.BlockSpec(memory_space=pltpu.VMEM)
    real = lambda *shape: jax.ShapeDtypeStruct(shape, jnp.float32)
    short = lambda *shape: jax.ShapeDtypeStruct(shape, density.dtype)

    cells = density.reshape(mats, planes, lines, blocks, LANES)
    rows = [lax.dynamic_index_in_dim(cells, end("tile", high, lines - 1), 2, keepdims=False) for high in (False, True)]
    tile_a = lax.ppermute(rows[0], AXES, partners("tile", 0))
    tile_b = lax.ppermute(rows[1], AXES, partners("tile", 1))

    def send(high, *before):
        return pl.pallas_call(
            functools.partial(plane_to_send, high),
            out_shape=short(mats, lines, blocks, LANES),
            in_specs=[vmem] + [pl.BlockSpec(memory_space=pl.ANY)] * len(before),
            out_specs=vmem,
            compiler_params=limit(2),
            cost_estimate=pl.CostEstimate(flops=1_000_000_000, bytes_accessed=2_000_000, transcendentals=0),
            name="plane_to_send",
        )(cells, *before)

    plane_b = send(True, *rows)
    depth_b = lax.ppermute(plane_b, AXES, partners("depth", 1))
    depth_a = lax.ppermute(send(False, plane_b), AXES, partners("depth", 0))
    hues, field, slope_x, half = pl.pallas_call(
        functools.partial(lookup, planes * depth),
        out_shape=(
            real(planes, lines * blocks // ROWS, 4 * energies, ROWS, LANES),
            real(*cells.shape),
            real(*cells.shape),
            real(energies * mats, ROWS, LANES),
        ),
        in_specs=[vmem] * 3,
        out_specs=(vmem,) * 4,
        scratch_shapes=[
            pltpu.VMEM((energies * mats, ROWS, LANES), jnp.float32),
            pltpu.VMEM((ROWS, LANES), jnp.int32),
            pltpu.VMEM((ROWS, LANES), jnp.int32),
        ],
        compiler_params=limit(8),
        cost_estimate=pl.CostEstimate(flops=4_000_000_000, bytes_accessed=8_000_000, transcendentals=300_000),
        name="lookup",
    )(material_weight, color_table, cells)
    half_kinds = 4 * energies
    tall = real(blocks * (half_kinds + 1) + 3 * ROWS, LANES)
    shared = (half, hues, field, slope_x, depth_a, depth_b)
    kept = sent = None
    for second, halo in ((False, tile_a), (True, tile_b)):
        filled = (kept, sent) if second else ()
        kept, sent = pl.pallas_call(
            functools.partial(shade, second),
            out_shape=(real(pairs, kinds, LANES),) * 2,
            in_specs=[vmem] * (7 + len(filled)),
            out_specs=(vmem, vmem),
            scratch_shapes=[pltpu.VMEM(tall.shape, jnp.float32)],
            input_output_aliases={7: 0, 8: 1} if second else {},
            compiler_params=limit(8),
            cost_estimate=pl.CostEstimate(flops=2_000_000_000, bytes_accessed=4_000_000, transcendentals=100_000),
            name="shade_second" if second else "shade_first",
        )(*shared, halo, *filled)
    other = lax.ppermute(sent, "depth", [(i, i ^ 1) for i in range(depth)])
    joined = pl.pallas_call(
        functools.partial(join, energies),
        out_shape=jax.ShapeDtypeStruct((pairs, kinds, LANES), jnp.int16),
        in_specs=[vmem, vmem],
        out_specs=vmem,
        compiler_params=limit(2),
        name="join",
    )(kept, other)
    same_core = [[2 * i + c for i in range(depth // 2)] for c in range(2)]
    parts = lax.all_to_all(joined, "depth", 0, 0, axis_index_groups=same_core, tiled=True)
    return pl.pallas_call(
        composite,
        out_shape=real(energies, 4, lines, columns // depth),
        in_specs=[vmem],
        out_specs=vmem,
        compiler_params=limit(2),
        name="composite",
    )(parts)


def solution(mesh):
    return jax.shard_map(
        body,
        mesh=mesh,
        in_specs=(P(None, "depth", "tile", None), P(), P()),
        out_specs=P(None, None, "tile", "depth"),
        check_vma=False,
    )
```
